32 devices in a mesh: group: 2 (over x), node: 2 (over core), local: 8 (over z, y).
Axes of the slice: x: 2, y: 2, z: 4, core: 2. Of those that a mesh axis runs over, the one named last changes fastest.
Arguments:
- query_rows: bfloat16 [6144, 2048], P(('group', 'node', 'local')), parts along dimension 0, may hold values from -6 to 6
- key_rows: bfloat16 [6144, 2048], P(('group', 'node', 'local')), parts along dimension 0, may hold values from -6 to 6
- value_rows: bfloat16 [6144, 2048], P(('group', 'node', 'local')), parts along dimension 0, may hold values from -6 to 6
- out_grad: bfloat16 [6144, 2048], P(('group', 'node', 'local')), parts along dimension 0, may hold values from -6 to 6
Outputs:
- attended: bfloat16 [6144, 2048], P(('group', 'node', 'local')), parts along dimension 0
- query_grad: bfloat16 [6144, 2048], P(('group', 'node', 'local')), parts along dimension 0
- key_grad: bfloat16 [6144, 2048], P(('group', 'node', 'local')), parts along dimension 0
- value_grad: bfloat16 [6144, 2048], P(('group', 'node', 'local')), parts along dimension 0
The draws below stay inside these ranges and needn't reach their ends.
There are 2 independent parts, one for each index of `group`. The reference program is written for one: setup_inputs(seed, part) draws one part's arguments, and reference() takes and returns one part's arrays. A program takes and returns all parts, laid end to end along the dimension named above; each array names one. Nothing has to cross between parts.
All inputs are finite; a program needn't handle non-finite values.
Results may differ from the reference program's by a relative error of at most 0.0051.
Values sent between devices are 32-bit elements; how exact they have to be, the bound alone decides.
No kernel may reach another device: no remote copies, remote signals or barrier semaphores. Data moves between devices by JAX's collectives and lax.ppermute only.
A program may use at most 320 MiB of HBM per device.

```python
import math
import jax
import jax.numpy as jnp
from jax import lax

HEADS = 16
HEAD_DIM = 128
TOK_DEV = 192
WIDTH = 2048
BLOCKS = 16
SEQ = 3072


def block_scale(rng, dims, split, low, largest):
    factor_of, own = 1.0, jax.random.fold_in(rng, 6)
    for position, blocks in split:
        heights = jnp.exp(jax.random.uniform(jax.random.fold_in(own, position), (blocks,), jnp.float32, low / len(split), largest / len(split)))
        factor_of = factor_of * jnp.repeat(heights, dims[position] // blocks).reshape([-1 if axis == position else 1 for axis in range(len(dims))])
    return factor_of


def bell_draw(own_key, extent, deviation, reach, split=(), kind=jnp.bfloat16):
    array = deviation * jax.random.normal(own_key, extent, jnp.float32)
    if split:
        array = array * block_scale(own_key, extent, split, -0.22, 0.18)
    return jnp.clip(array, -reach, reach).astype(kind)


def setup_inputs(seed: int = 0, part: int = 0) -> dict:
    splits = jax.random.split(jax.random.key(seed), 5)
    part_splits = jax.random.split(jax.random.fold_in(splits[4], part), 5)
    return {
        "query_rows": bell_draw(part_splits[0], (SEQ, WIDTH), 1.0, 6.0, ((0, 16),)),
        "key_rows": bell_draw(part_splits[1], (SEQ, WIDTH), 1.0, 6.0, ((0, 16),)),
        "value_rows": bell_draw(part_splits[2], (SEQ, WIDTH), 1.0, 6.0, ((0, 16),)),
        "out_grad": bell_draw(part_splits[3], (SEQ, WIDTH), 1.0, 6.0, ((0, 16),)),
    }


def to_low(values):
    return lax.optimization_barrier(values.astype(jnp.bfloat16)).astype(jnp.float32)

def block_terms(pieces):
    query_heads, key_heads, value_heads, grad_heads, prefix, suffix = pieces
    factor = 1.0 / math.sqrt(HEAD_DIM * SEQ)
    queries = query_heads.astype(jnp.float32)
    keyset = key_heads.astype(jnp.float32)
    valueset = value_heads.astype(jnp.float32)
    gradset = grad_heads.astype(jnp.float32)
    causal = jnp.tril(jnp.ones((TOK_DEV, TOK_DEV), dtype=bool))
    prefix_low = to_low(prefix)
    suffix_low = to_low(suffix)
    scores = jnp.einsum('thd,shd->hts', queries, keyset)
    weights = to_low(jnp.where(causal[None], scores, 0.0))
    grad_scores = jnp.einsum('the,she->hts', gradset, valueset)
    grad_weights = to_low(jnp.where(causal[None], grad_scores, 0.0))
    attended = jnp.einsum('hts,she->the', weights, valueset) + jnp.einsum('thd,hde->the', queries, prefix_low)
    query_grad = jnp.einsum('hts,shd->thd', grad_weights, keyset) + jnp.einsum('the,hde->thd', gradset, prefix_low)
    key_grad = jnp.einsum('hts,thd->shd', grad_weights, queries) + jnp.einsum('she,hde->shd', valueset, suffix_low)
    value_grad = jnp.einsum('hts,the->she', weights, gradset) + jnp.einsum('shd,hde->she', keyset, suffix_low)
    return tuple(((factor * item).astype(jnp.bfloat16).reshape(TOK_DEV, WIDTH) for item in (attended, query_grad, key_grad, value_grad)))

def reference(query_rows, key_rows, value_rows, out_grad):
    shape = (BLOCKS, TOK_DEV, HEADS, HEAD_DIM)
    query_heads = query_rows.reshape(shape)
    key_heads = key_rows.reshape(shape)
    value_heads = value_rows.reshape(shape)
    grad_heads = out_grad.reshape(shape)
    key_state = jnp.einsum('bthd,bthe->bhde', key_heads.astype(jnp.float32), value_heads.astype(jnp.float32))
    grad_state = jnp.einsum('bthd,bthe->bhde', query_heads.astype(jnp.float32), grad_heads.astype(jnp.float32))
    blank = jnp.zeros_like(key_state[:1])
    prefix = jnp.cumsum(jnp.concatenate([blank, key_state[:-1]], axis=0), axis=0)
    shifted = jnp.concatenate([grad_state[1:], blank], axis=0)
    suffix = jnp.cumsum(shifted[::-1], axis=0)[::-1]
    results = lax.map(block_terms, (query_heads, key_heads, value_heads, grad_heads, prefix, suffix))
    return tuple((item.reshape(SEQ, WIDTH) for item in results))
```

```python
import functools
import math

import jax
import jax.numpy as jnp
from jax import lax
from jax.experimental import pallas as pl
from jax.experimental.pallas import tpu as pltpu
from jax.sharding import PartitionSpec as P

HEAD_DIM = 128
PARTS = 4
QUARTER = HEAD_DIM // PARTS
CHUNKS = (8, 8)
STEP = 4

F32 = jnp.float32
BF16 = jnp.bfloat16
VMEM_LIMIT = 40 * 1024 * 1024


def dot(a, b, ca, cb):
    return lax.dot_general(a, b, (((ca,), (cb,)), ((), ())), preferred_element_type=F32)


def place(info, r):
    return pl.multiple_of((info[0] ^ r) * QUARTER, QUARTER)


def state_kernel(step, info, q, k, v, g, *refs):
    outs, hold = refs[:PARTS], refs[PARTS]
    for h in range(step):
        cols = slice(h * HEAD_DIM, (h + 1) * HEAD_DIM)
        hold[0] = dot(k[:, cols], v[:, cols], 0, 0)
        hold[1] = dot(q[:, cols], g[:, cols], 0, 0)
        for r in range(PARTS):
            rows = pl.ds(place(info, r), QUARTER)
            outs[r][0, h] = hold[0, rows, :]
            outs[r][1, h] = hold[1, rows, :]


def states(info, arrays, first, heads, step):
    rows = arrays[0].shape[0]
    piece = jax.ShapeDtypeStruct((2, heads, QUARTER, HEAD_DIM), F32)
    return pl.pallas_call(
        functools.partial(state_kernel, step),
        out_shape=[piece] * PARTS,
        grid_spec=pltpu.PrefetchScalarGridSpec(
            num_scalar_prefetch=1,
            grid=(heads // step,),
            in_specs=[
                pl.BlockSpec((rows, step * HEAD_DIM), lambda i, info: (0, first // step + i))
            ]
            * 4,
            out_specs=[
                pl.BlockSpec((2, step, QUARTER, HEAD_DIM), lambda i, info: (0, i, 0, 0))
            ]
            * PARTS,
            scratch_shapes=[pltpu.VMEM((2, HEAD_DIM, HEAD_DIM), F32)],
        ),
        compiler_params=pltpu.CompilerParams(vmem_limit_bytes=VMEM_LIMIT),
        cost_estimate=pl.CostEstimate(
            flops=4 * heads * rows * HEAD_DIM * HEAD_DIM,
            bytes_accessed=heads * (8 * rows * HEAD_DIM + 8 * HEAD_DIM * HEAD_DIM),
            transcendentals=0,
        ),
    )(info, *arrays)


def spread_kernel(levels, info, *refs):
    pieces = refs[:PARTS]
    totals = refs[PARTS : PARTS + levels]
    across = refs[PARTS + levels]
    outs = refs[PARTS + levels + 1 :]
    mine, node, block = info[0], info[1], info[2]
    prefix = jnp.where(node > 0, across[...], 0.0)
    suffix = jnp.where(node > 0, 0.0, across[...])
    for level in range(levels):
        upper = ((block >> level) & 1) > 0
        prefix = prefix + jnp.where(upper, totals[level][0], 0.0)
        suffix = suffix + jnp.where(upper, 0.0, totals[level][1])
    for r in range(PARTS):
        before, after = prefix, suffix
        for other in range(PARTS):
            if other != r:
                earlier = (mine ^ other) < (mine ^ r)
                before = before + jnp.where(earlier, pieces[other][0], 0.0)
                after = after + jnp.where(earlier, 0.0, pieces[other][1])
        outs[r][0] = before
        outs[r][1] = after


def spread(info, pieces, totals, across):
    levels = len(totals)
    whole = pl.BlockSpec(memory_space=pltpu.VMEM)
    size = pieces[0].size * 4
    return pl.pallas_call(
        functools.partial(spread_kernel, levels),
        out_shape=[jax.ShapeDtypeStruct(pieces[0].shape, F32)] * PARTS,
        in_specs=[pl.BlockSpec(memory_space=pltpu.SMEM)] + [whole] * (PARTS + levels + 1),
        out_specs=[whole] * PARTS,
        compiler_params=pltpu.CompilerParams(vmem_limit_bytes=VMEM_LIMIT),
        cost_estimate=pl.CostEstimate(
            flops=pieces[0].size * 30,
            bytes_accessed=size * (2 * PARTS + levels + 1),
            transcendentals=0,
        ),
    )(info, *pieces, *totals, across)


def finish_kernel(step, factor, info, q, k, v, g, *refs):
    pieces, (att, qg, kg, vg), hold = refs[:PARTS], refs[-5:-1], refs[-1]
    rows = q.shape[0]
    causal = lax.broadcasted_iota(jnp.int32, (rows, rows), 0) >= lax.broadcasted_iota(
        jnp.int32, (rows, rows), 1
    )
    for h in range(step):
        cols = slice(h * HEAD_DIM, (h + 1) * HEAD_DIM)
        for r in range(PARTS):
            at = pl.ds(place(info, r), QUARTER)
            hold[0, at, :] = pieces[r][0, h].astype(BF16)
            hold[1, at, :] = pieces[r][1, h].astype(BF16)
        qh, kh, vh, gh = q[:, cols], k[:, cols], v[:, cols], g[:, cols]
        prefix, suffix = hold[0], hold[1]
        weights = jnp.where(causal, dot(qh, kh, 1, 1), 0.0).astype(BF16)
        grad_weights = jnp.where(causal, dot(gh, vh, 1, 1), 0.0).astype(BF16)
        att[:, cols] = (factor * (dot(weights, vh, 1, 0) + dot(qh, prefix, 1, 0))).astype(BF16)
        qg[:, cols] = (factor * (dot(grad_weights, kh, 1, 0) + dot(gh, prefix, 1, 1))).astype(BF16)
        kg[:, cols] = (factor * (dot(grad_weights, qh, 0, 0) + dot(vh, suffix, 1, 1))).astype(BF16)
        vg[:, cols] = (factor * (dot(weights, gh, 0, 0) + dot(kh, suffix, 1, 0))).astype(BF16)


def finish(info, arrays, pieces, outs, first, step, factor):
    rows, width = arrays[0].shape
    heads = pieces[0].shape[1]
    columns = pl.BlockSpec((rows, step * HEAD_DIM), lambda i, info: (0, first // step + i))
    quarter = pl.BlockSpec((2, step, QUARTER, HEAD_DIM), lambda i, info: (0, i, 0, 0))
    given = [info, *arrays, *pieces, *outs]
    fixed = 5 + PARTS
    return pl.pallas_call(
        functools.partial(finish_kernel, step, factor),
        out_shape=[jax.ShapeDtypeStruct((rows, width), BF16)] * 4,
        grid_spec=pltpu.PrefetchScalarGridSpec(
            num_scalar_prefetch=1,
            grid=(heads // step,),
            in_specs=[columns] * 4
            + [quarter] * PARTS
            + [pl.BlockSpec(memory_space=pl.ANY)] * len(outs),
            out_specs=[columns] * 4,
            scratch_shapes=[pltpu.VMEM((2, HEAD_DIM, HEAD_DIM), BF16)],
        ),
        input_output_aliases={fixed + i: i for i in range(len(outs))},
        compiler_params=pltpu.CompilerParams(vmem_limit_bytes=VMEM_LIMIT),
        cost_estimate=pl.CostEstimate(
            flops=heads * rows * HEAD_DIM * (12 * rows + 8 * HEAD_DIM),
            bytes_accessed=heads * HEAD_DIM * (16 * rows + 8 * HEAD_DIM),
            transcendentals=0,
        ),
    )(*given)


def swap(array, size, mask):
    return lax.ppermute(array, "local", [(i, i ^ mask) for i in range(size)])


def local(query_rows, key_rows, value_rows, out_grad):
    arrays = (query_rows, key_rows, value_rows, out_grad)
    rows, width = query_rows.shape
    heads = width // HEAD_DIM
    size, nodes = lax.axis_size("local"), lax.axis_size("node")
    blocks = size // PARTS
    levels = blocks.bit_length() - 1
    assert nodes == 2 and PARTS << levels == size and sum(CHUNKS) == heads
    factor = 1.0 / math.sqrt(HEAD_DIM * rows * nodes * size)
    node, place_in = lax.axis_index("node"), lax.axis_index("local")
    info = jnp.stack([place_in % PARTS, node, place_in // PARTS]).astype(jnp.int32)

    firsts = [sum(CHUNKS[:i]) for i in range(len(CHUNKS))]
    outs = ()
    gathered = []
    for first, count in zip(firsts, CHUNKS):
        own = states(info, arrays, first, count, STEP)
        gathered.append([own[0]] + [swap(own[r], size, r) for r in (1, 3, 2)])
    returned = []
    for got in gathered:
        pieces = [got[0], got[1], got[3], got[2]]
        total = (pieces[0] + pieces[1]) + (pieces[2] + pieces[3])
        totals = []
        for level in range(levels):
            totals.append(swap(total, size, PARTS << level))
            total = total + totals[-1]
        across = lax.ppermute(
            jnp.where(node > 0, total[1], total[0]), "node", [(0, 1), (1, 0)]
        )
        ready = spread(info, pieces, totals, across)
        back = [swap(ready[r], size, r) for r in (1, 3, 2)]
        returned.append([ready[0], back[0], back[2], back[1]])
    for first, pieces in zip(firsts, returned):
        outs = finish(info, arrays, pieces, outs, first, STEP, factor)
    return tuple(outs)


def solution(mesh):
    rows = P(("group", "node", "local"), None)
    return jax.shard_map(
        local, mesh=mesh, in_specs=(rows,) * 4, out_specs=(rows,) * 4, check_vma=False
    )
```

```python
import functools
import math

import jax
import jax.numpy as jnp
from jax import lax
from jax.experimental import pallas as pl
from jax.experimental.pallas import tpu as pltpu
from jax.sharding import PartitionSpec as P

HEAD_DIM = 128
PARTS = 4
QUARTER = HEAD_DIM // PARTS
CHUNKS = (8, 8)
STEP = 4
FINISH_STEP = (4, 4)
ORDER = (
    ("state", 0),
    ("state", 1),
    ("sum", 0),
    ("sum", 1),
    ("half", 0),
    ("spread", 0),
    ("half", 1),
    ("spread", 1, (0, 1), (0, 2), (0, 3)),
    ("finish", 0),
    ("finish", 1),
)

F32 = jnp.float32
BF16 = jnp.bfloat16
VMEM_LIMIT = 40 * 1024 * 1024
STATE_LIMIT = 60 * 1024 * 1024

LIGHT = pl.CostEstimate(flops=1, bytes_accessed=1, transcendentals=0)
SCALARS = pl.BlockSpec(memory_space=pltpu.SMEM)
WHOLE = pl.BlockSpec(memory_space=pltpu.VMEM)
FAR = pl.BlockSpec(memory_space=pltpu.HBM)
LEFT = pl.BlockSpec(memory_space=pl.ANY)


def dot(a, b, ca, cb):
    return lax.dot_general(a, b, (((ca,), (cb,)), ((), ())), preferred_element_type=F32)


def place(info, r):
    return pl.multiple_of((info[0] ^ r) * QUARTER, QUARTER)


def state_kernel(first, heads, info, q, k, v, g, *refs):
    outs, (held, hold, sems) = refs[-PARTS - 3 : -3], refs[-3:]
    groups = [(at, min(STEP, heads - at)) for at in range(0, heads, STEP)]
    copies = []
    for n, (at, wide) in enumerate(groups):
        there = pl.ds((first + at) * HEAD_DIM, wide * HEAD_DIM)
        here = pl.ds(at * HEAD_DIM, wide * HEAD_DIM)
        copies.append(
            [
                pltpu.make_async_copy(ref.at[:, there], held.at[i, :, here], sems.at[n, i])
                for i, ref in enumerate((k, v, q, g))
            ]
        )
        for copy in copies[-1]:
            copy.start()
    for n, (at, wide) in enumerate(groups):
        for half in range(2):
            copies[n][2 * half].wait()
            copies[n][2 * half + 1].wait()
            for h in range(at, at + wide):
                cols = slice(h * HEAD_DIM, (h + 1) * HEAD_DIM)
                hold[half] = dot(held[2 * half, :, cols], held[2 * half + 1, :, cols], 0, 0)
                for r in range(PARTS):
                    outs[r][half, h] = hold[half, pl.ds(place(info, r), QUARTER), :]


def states(info, arrays, first, heads, behind):
    rows = arrays[0].shape[0]
    piece = jax.ShapeDtypeStruct((2, heads, QUARTER, HEAD_DIM), F32)
    return pl.pallas_call(
        functools.partial(state_kernel, first, heads),
        out_shape=[piece] * PARTS,
        in_specs=[SCALARS] + [FAR] * 4 + [LEFT] * len(behind),
        out_specs=[WHOLE] * PARTS,
        scratch_shapes=[
            pltpu.VMEM((4, rows, heads * HEAD_DIM), BF16),
            pltpu.VMEM((2, HEAD_DIM, HEAD_DIM), F32),
            pltpu.SemaphoreType.DMA((-(-heads // STEP), 4)),
        ],
        compiler_params=pltpu.CompilerParams(vmem_limit_bytes=STATE_LIMIT),
        cost_estimate=LIGHT,
    )(info, *arrays, *behind)


def sum_kernel(a, b, c, d, *refs):
    refs[-1][...] = (a[...] + b[...]) + (c[...] + d[...])


def block_sum(pieces, behind):
    shape = jax.ShapeDtypeStruct(pieces[0].shape, F32)
    return pl.pallas_call(
        sum_kernel,
        out_shape=shape,
        in_specs=[WHOLE] * PARTS + [LEFT] * len(behind),
        out_specs=WHOLE,
        compiler_params=pltpu.CompilerParams(vmem_limit_bytes=VMEM_LIMIT),
        cost_estimate=LIGHT,
    )(*pieces, *behind)


def across_kernel(info, a, b, *refs):
    take = jnp.where(info[1] > 0, 1, 0)
    refs[-1][...] = a[take] + b[take]


def half_total(info, total, other, behind):
    shape = jax.ShapeDtypeStruct(total.shape[1:], F32)
    return pl.pallas_call(
        across_kernel,
        out_shape=shape,
        in_specs=[SCALARS, WHOLE, WHOLE] + [LEFT] * len(behind),
        out_specs=WHOLE,
        compiler_params=pltpu.CompilerParams(vmem_limit_bytes=VMEM_LIMIT),
        cost_estimate=LIGHT,
    )(info, total, other, *behind)


def spread_kernel(levels, info, *refs):
    pieces = refs[:PARTS]
    totals = refs[PARTS : PARTS + levels]
    across = refs[PARTS + levels]
    outs = refs[-PARTS:]
    mine, node, block = info[0], info[1], info[2]
    prefix = jnp.where(node > 0, across[...], 0.0)
    suffix = jnp.where(node > 0, 0.0, across[...])
    for level in range(levels):
        upper = ((block >> level) & 1) > 0
        prefix = prefix + jnp.where(upper, totals[level][0], 0.0)
        suffix = suffix + jnp.where(upper, 0.0, totals[level][1])
    for r in range(PARTS):
        before, after = prefix, suffix
        for other in range(PARTS):
            if other != r:
                earlier = (mine ^ other) < (mine ^ r)
                before = before + jnp.where(earlier, pieces[other][0], 0.0)
                after = after + jnp.where(earlier, 0.0, pieces[other][1])
        outs[r][0] = before
        outs[r][1] = after


def spread(info, pieces, totals, across, behind):
    levels = len(totals)
    shapes = [jax.ShapeDtypeStruct(pieces[0].shape, F32)] * PARTS
    return pl.pallas_call(
        functools.partial(spread_kernel, levels),
        out_shape=shapes,
        in_specs=[SCALARS] + [WHOLE] * (PARTS + levels + 1) + [LEFT] * len(behind),
        out_specs=[WHOLE] * PARTS,
        compiler_params=pltpu.CompilerParams(vmem_limit_bytes=VMEM_LIMIT),
        cost_estimate=LIGHT,
    )(info, *pieces, *totals, across, *behind)


def finish_kernel(step, factor, info, q, k, v, g, *refs):
    pieces, (att, qg, kg, vg), hold = refs[:PARTS], refs[-5:-1], refs[-1]
    rows = q.shape[0]
    causal = lax.broadcasted_iota(jnp.int32, (rows, rows), 0) >= lax.broadcasted_iota(
        jnp.int32, (rows, rows), 1
    )
    for h in range(step):
        cols = slice(h * HEAD_DIM, (h + 1) * HEAD_DIM)
        for r in range(PARTS):
            at = pl.ds(place(info, r), QUARTER)
            hold[0, at, :] = pieces[r][0, h].astype(BF16)
            hold[1, at, :] = pieces[r][1, h].astype(BF16)
        qh, kh, vh, gh = q[:, cols], k[:, cols], v[:, cols], g[:, cols]
        prefix, suffix = hold[0], hold[1]
        weights = jnp.where(causal, dot(qh, kh, 1, 1), 0.0).astype(BF16)
        grad_weights = jnp.where(causal, dot(gh, vh, 1, 1), 0.0).astype(BF16)
        att[:, cols] = (factor * (dot(weights, vh, 1, 0) + dot(qh, prefix, 1, 0))).astype(BF16)
        qg[:, cols] = (factor * (dot(grad_weights, kh, 1, 0) + dot(gh, prefix, 1, 1))).astype(BF16)
        kg[:, cols] = (factor * (dot(grad_weights, qh, 0, 0) + dot(vh, suffix, 1, 1))).astype(BF16)
        vg[:, cols] = (factor * (dot(weights, gh, 0, 0) + dot(kh, suffix, 1, 0))).astype(BF16)


def finish(info, arrays, pieces, outs, first, step, factor, behind):
    rows, width = arrays[0].shape
    heads = pieces[0].shape[1]
    columns = pl.BlockSpec((rows, step * HEAD_DIM), lambda i, info: (0, first // step + i))
    quarter = pl.BlockSpec((2, step, QUARTER, HEAD_DIM), lambda i, info: (0, i, 0, 0))
    given = [info, *arrays, *pieces, *outs, *behind]
    fixed = 5 + PARTS
    return pl.pallas_call(
        functools.partial(finish_kernel, step, factor),
        out_shape=[jax.ShapeDtypeStruct((rows, width), BF16)] * 4,
        grid_spec=pltpu.PrefetchScalarGridSpec(
            num_scalar_prefetch=1,
            grid=(heads // step,),
            in_specs=[columns] * 4
            + [quarter] * PARTS
            + [LEFT] * (len(outs) + len(behind)),
            out_specs=[columns] * 4,
            scratch_shapes=[pltpu.VMEM((2, HEAD_DIM, HEAD_DIM), BF16)],
        ),
        input_output_aliases={fixed + i: i for i in range(len(outs))},
        compiler_params=pltpu.CompilerParams(vmem_limit_bytes=VMEM_LIMIT),
        cost_estimate=LIGHT,
    )(*given)


def swap(array, size, mask):
    return lax.ppermute(array, "local", [(i, i ^ mask) for i in range(size)])


def local(query_rows, key_rows, value_rows, out_grad):
    arrays = (query_rows, key_rows, value_rows, out_grad)
    rows, width = query_rows.shape
    heads = width // HEAD_DIM
    size, nodes = lax.axis_size("local"), lax.axis_size("node")
    blocks = size // PARTS
    levels = blocks.bit_length() - 1
    assert nodes == 2 and PARTS << levels == size and sum(CHUNKS) == heads
    factor = 1.0 / math.sqrt(HEAD_DIM * rows * nodes * size)
    node, place_in = lax.axis_index("node"), lax.axis_index("local")
    info = jnp.stack([place_in % PARTS, node, place_in // PARTS]).astype(jnp.int32)

    firsts = [sum(CHUNKS[:i]) for i in range(len(CHUNKS))]
    done = {}
    outs = ()
    last = info
    for stage, i, *after in ORDER:
        first, count = firsts[i], CHUNKS[i]
        behind = [last] + [done["ready", j][r] for j, r in after]
        if stage == "state":
            own = states(info, arrays, first, count, behind)
            last = own[0]
            got = {r: swap(own[r], size, r) for r in (1, 3, 2)}
            done["pieces", i] = [own[0], got[1], got[2], got[3]]
        elif stage == "sum":
            last = total = block_sum(done["pieces", i], behind)
            totals = []
            for level in range(levels):
                if level:
                    total = total + totals[-1]
                totals.append(swap(total, size, PARTS << level))
            done["totals", i] = total, totals
        elif stage == "half":
            total, totals = done["totals", i]
            last = half_total(info, total, totals[-1], behind)
            done["across", i] = lax.ppermute(last, "node", [(0, 1), (1, 0)])
        elif stage == "spread":
            ready = spread(info, done["pieces", i], done["totals", i][1], done["across", i], behind)
            last = ready[0]
            back = {r: swap(ready[r], size, r) for r in (1, 3, 2)}
            done["ready", i] = [ready[0], back[1], back[2], back[3]]
        else:
            outs = finish(info, arrays, done["ready", i], outs, first, FINISH_STEP[i], factor, behind)
    return tuple(outs)


def solution(mesh):
    rows = P(("group", "node", "local"), None)
    return jax.shard_map(
        local, mesh=mesh, in_specs=(rows,) * 4, out_specs=(rows,) * 4, check_vma=False
    )
```

```python
import functools
import math

import jax
import jax.numpy as jnp
from jax import lax
from jax.experimental import pallas as pl
from jax.experimental.pallas import tpu as pltpu
from jax.sharding import PartitionSpec as P

HEAD_DIM = 128
PARTS = 4
QUARTER = HEAD_DIM // PARTS
CHUNKS = (8, 8)
STEP = 4
FINISH_STEP = (4, 4)
ORDER = (
    ("state", 0),
    ("state", 1),
    ("sum", 0),
    ("offer", 0),
    ("sum", 1),
    ("offer", 1),
    ("spread", 0),
    ("spread", 1),
    ("finish", 0),
    ("finish", 1),
)

F32 = jnp.float32
BF16 = jnp.bfloat16
VMEM_LIMIT = 40 * 1024 * 1024
STATE_LIMIT = 60 * 1024 * 1024

SCALARS = pl.BlockSpec(memory_space=pltpu.SMEM)
WHOLE = pl.BlockSpec(memory_space=pltpu.VMEM)
FAR = pl.BlockSpec(memory_space=pltpu.HBM)
LEFT = pl.BlockSpec(memory_space=pl.ANY)


def dot(a, b, ca, cb):
    return lax.dot_general(a, b, (((ca,), (cb,)), ((), ())), preferred_element_type=F32)


def place(info, r):
    return pl.multiple_of((info[0] ^ r) * QUARTER, QUARTER)


def state_kernel(first, heads, info, q, k, v, g, *refs):
    outs, (held, hold, sems) = refs[-PARTS - 3 : -3], refs[-3:]
    groups = [(at, min(STEP, heads - at)) for at in range(0, heads, STEP)]
    copies = []
    for n, (at, wide) in enumerate(groups):
        there = pl.ds((first + at) * HEAD_DIM, wide * HEAD_DIM)
        here = pl.ds(at * HEAD_DIM, wide * HEAD_DIM)
        copies.append(
            [
                pltpu.make_async_copy(ref.at[:, there], held.at[i, :, here], sems.at[n, i])
                for i, ref in enumerate((k, v, q, g))
            ]
        )
        for copy in copies[-1]:
            copy.start()
    for n, (at, wide) in enumerate(groups):
        for half in range(2):
            copies[n][2 * half].wait()
            copies[n][2 * half + 1].wait()
            for h in range(at, at + wide):
                cols = slice(h * HEAD_DIM, (h + 1) * HEAD_DIM)
                hold[half] = dot(held[2 * half, :, cols], held[2 * half + 1, :, cols], 0, 0)
                for r in range(PARTS):
                    outs[r][half, h] = hold[half, pl.ds(place(info, r), QUARTER), :]


def states(info, arrays, first, heads, behind):
    rows = arrays[0].shape[0]
    piece = jax.ShapeDtypeStruct((2, heads, QUARTER, HEAD_DIM), F32)
    return pl.pallas_call(
        functools.partial(state_kernel, first, heads),
        out_shape=[piece] * PARTS,
        in_specs=[SCALARS] + [FAR] * 4 + [LEFT] * len(behind),
        out_specs=[WHOLE] * PARTS,
        scratch_shapes=[
            pltpu.VMEM((4, rows, heads * HEAD_DIM), BF16),
            pltpu.VMEM((2, HEAD_DIM, HEAD_DIM), F32),
            pltpu.SemaphoreType.DMA((-(-heads // STEP), 4)),
        ],
        compiler_params=pltpu.CompilerParams(vmem_limit_bytes=STATE_LIMIT),
    )(info, *arrays, *behind)


def add_kernel(info, a, b, c, d, *refs):
    total, halves = refs[-2:]
    total[...] = (a[...] + b[...]) + (c[...] + d[...])
    halves[...] = total[info[1]]


def block_sum(info, pieces, behind):
    shape = pieces[0].shape
    return pl.pallas_call(
        add_kernel,
        out_shape=[jax.ShapeDtypeStruct(shape, F32), jax.ShapeDtypeStruct(shape[1:], F32)],
        in_specs=[SCALARS] + [WHOLE] * PARTS + [LEFT] * len(behind),
        out_specs=[WHOLE] * 2,
        compiler_params=pltpu.CompilerParams(vmem_limit_bytes=VMEM_LIMIT),
    )(info, *pieces, *behind)


def offer_kernel(info, total, across, *refs):
    out = refs[-1]
    upper = info[2] > 0
    whole = 1 - info[1]
    other = info[1]
    send = jnp.logical_xor(upper, whole == 0)
    out[other] = total[other]
    out[whole] = across[...] + jnp.where(send, total[whole], 0.0)


def offer(info, total, across, behind):
    return pl.pallas_call(
        offer_kernel,
        out_shape=jax.ShapeDtypeStruct(total.shape, F32),
        in_specs=[SCALARS, WHOLE, WHOLE] + [LEFT] * len(behind),
        out_specs=WHOLE,
        compiler_params=pltpu.CompilerParams(vmem_limit_bytes=VMEM_LIMIT),
    )(info, total, across, *behind)


def spread_kernel(pair, info, *refs):
    pieces, given, outs = refs[:PARTS], refs[PARTS : PARTS + 1 + pair], refs[-PARTS:]
    mine, node, upper = info[0], info[1], info[2] > 0
    if pair:
        across, other = given
        late = node > 0
        prefix = jnp.where(late, across[...], 0.0) + jnp.where(late | upper, other[0], 0.0)
        suffix = jnp.where(late, 0.0, across[...]) + jnp.where(late & upper, 0.0, other[1])
    else:
        prefix, suffix = given[0][0], given[0][1]
    for r in range(PARTS):
        before, after = prefix, suffix
        for other in range(PARTS):
            if other != r:
                earlier = (mine ^ other) < (mine ^ r)
                before = before + jnp.where(earlier, pieces[other][0], 0.0)
                after = after + jnp.where(earlier, 0.0, pieces[other][1])
        outs[r][0] = before
        outs[r][1] = after


def spread(info, pieces, given, behind):
    return pl.pallas_call(
        functools.partial(spread_kernel, len(given) > 1),
        out_shape=[jax.ShapeDtypeStruct(pieces[0].shape, F32)] * PARTS,
        in_specs=[SCALARS] + [WHOLE] * (PARTS + len(given)) + [LEFT] * len(behind),
        out_specs=[WHOLE] * PARTS,
        compiler_params=pltpu.CompilerParams(vmem_limit_bytes=VMEM_LIMIT),
    )(info, *pieces, *given, *behind)


def sums_outside(total, node, block, blocks):
    everything = lax.all_gather(total, ("node", "local"))
    everything = everything.reshape(-1, blocks, PARTS, *total.shape)
    everything = lax.dynamic_index_in_dim(everything, lax.axis_index("local") % PARTS, 2, False)
    everything = everything.reshape(-1, *total.shape)
    at = node * blocks + block
    earlier = (jnp.arange(everything.shape[0]) < at)[:, None, None, None]
    later = (jnp.arange(everything.shape[0]) > at)[:, None, None, None]
    prefix = jnp.sum(jnp.where(earlier, everything[:, 0], 0.0), axis=0)
    suffix = jnp.sum(jnp.where(later, everything[:, 1], 0.0), axis=0)
    return jnp.stack([prefix, suffix])


def finish_kernel(step, factor, info, q, k, v, g, *refs):
    pieces, (att, qg, kg, vg), hold = refs[:PARTS], refs[-5:-1], refs[-1]
    rows = q.shape[0]
    causal = lax.broadcasted_iota(jnp.int32, (rows, rows), 0) >= lax.broadcasted_iota(
        jnp.int32, (rows, rows), 1
    )
    for h in range(step):
        cols = slice(h * HEAD_DIM, (h + 1) * HEAD_DIM)
        for r in range(PARTS):
            at = pl.ds(place(info, r), QUARTER)
            hold[0, at, :] = pieces[r][0, h].astype(BF16)
            hold[1, at, :] = pieces[r][1, h].astype(BF16)
        qh, kh, vh, gh = q[:, cols], k[:, cols], v[:, cols], g[:, cols]
        prefix, suffix = hold[0], hold[1]
        weights = jnp.where(causal, dot(qh, kh, 1, 1), 0.0).astype(BF16)
        grad_weights = jnp.where(causal, dot(gh, vh, 1, 1), 0.0).astype(BF16)
        att[:, cols] = (factor * (dot(weights, vh, 1, 0) + dot(qh, prefix, 1, 0))).astype(BF16)
        qg[:, cols] = (factor * (dot(grad_weights, kh, 1, 0) + dot(gh, prefix, 1, 1))).astype(BF16)
        kg[:, cols] = (factor * (dot(grad_weights, qh, 0, 0) + dot(vh, suffix, 1, 1))).astype(BF16)
        vg[:, cols] = (factor * (dot(weights, gh, 0, 0) + dot(kh, suffix, 1, 0))).astype(BF16)


def finish(info, arrays, pieces, outs, first, step, factor, behind):
    rows, width = arrays[0].shape
    heads = pieces[0].shape[1]
    columns = pl.BlockSpec((rows, step * HEAD_DIM), lambda i, info: (0, first // step + i))
    quarter = pl.BlockSpec((2, step, QUARTER, HEAD_DIM), lambda i, info: (0, i, 0, 0))
    given = [info, *arrays, *pieces, *outs, *behind]
    fixed = 5 + PARTS
    return pl.pallas_call(
        functools.partial(finish_kernel, step, factor),
        out_shape=[jax.ShapeDtypeStruct((rows, width), BF16)] * 4,
        grid_spec=pltpu.PrefetchScalarGridSpec(
            num_scalar_prefetch=1,
            grid=(heads // step,),
            in_specs=[columns] * 4
            + [quarter] * PARTS
            + [LEFT] * (len(outs) + len(behind)),
            out_specs=[columns] * 4,
            scratch_shapes=[pltpu.VMEM((2, HEAD_DIM, HEAD_DIM), BF16)],
        ),
        input_output_aliases={fixed + i: i for i in range(len(outs))},
        compiler_params=pltpu.CompilerParams(vmem_limit_bytes=VMEM_LIMIT),
    )(*given)


def swap(array, size, mask):
    return lax.ppermute(array, "local", [(i, i ^ mask) for i in range(size)])


def local(query_rows, key_rows, value_rows, out_grad):
    arrays = (query_rows, key_rows, value_rows, out_grad)
    rows, width = query_rows.shape
    heads = width // HEAD_DIM
    size, nodes = lax.axis_size("local"), lax.axis_size("node")
    blocks = size // PARTS
    assert nodes == 2 and size % PARTS == 0 and sum(CHUNKS) == heads
    factor = 1.0 / math.sqrt(HEAD_DIM * rows * nodes * size)
    node, place_in = lax.axis_index("node"), lax.axis_index("local")
    info = jnp.stack([place_in % PARTS, node, place_in // PARTS]).astype(jnp.int32)

    firsts = [sum(CHUNKS[:i]) for i in range(len(CHUNKS))]
    pieces, given, ready, state = {}, {}, {}, {}
    outs = ()
    last = info
    for stage, i in ORDER:
        first, count = firsts[i], CHUNKS[i]
        behind = [last]
        if stage == "state":
            own = states(info, arrays, first, count, behind)
            last = own[0]
            got = {r: swap(own[r], size, r) for r in (1, 3, 2)}
            pieces[i] = [own[0], got[1], got[2], got[3]]
        elif stage == "sum":
            last, halves = block_sum(info, pieces[i], behind)
            across = lax.ppermute(halves, "node", [(0, 1), (1, 0)])
            state[i] = last, across
        elif stage == "offer":
            total, across = state[i]
            if blocks == 2:
                last = offer(info, total, across, behind)
                given[i] = [across, swap(last, size, PARTS)]
            else:
                given[i] = [sums_outside(total, node, place_in // PARTS, blocks)]
        elif stage == "spread":
            own = spread(info, pieces[i], given[i], behind)
            last = own[0]
            got = {r: swap(own[r], size, r) for r in (1, 3, 2)}
            ready[i] = [own[0], got[1], got[2], got[3]]
        else:
            outs = finish(info, arrays, ready[i], outs, first, FINISH_STEP[i], factor, behind)
    return tuple(outs)


def solution(mesh):
    rows = P(("group", "node", "local"), None)
    return jax.shard_map(
        local, mesh=mesh, in_specs=(rows,) * 4, out_specs=(rows,) * 4, check_vma=False
    )
```

```python
import functools
import math

import jax
import jax.numpy as jnp
from jax import lax
from jax.experimental import pallas as pl
from jax.experimental.pallas import tpu as pltpu
from jax.sharding import PartitionSpec as P

HEAD_DIM = 128
PARTS = 4
QUARTER = HEAD_DIM // PARTS
CHUNKS = (8, 8)
STEP = 8
FINISH_STEP = (4, 4)
ORDER = (
    ("state", 0),
    ("state", 1),
    ("inner", 0),
    ("sum", 0),
    ("offer", 0),
    ("inner", 1),
    ("sum", 1),
    ("offer", 1),
    ("spread", 0),
    ("spread", 1),
    ("finish", 0),
    ("finish", 1),
)

F32 = jnp.float32
BF16 = jnp.bfloat16
VMEM_LIMIT = 40 * 1024 * 1024
SMALL_LIMIT = 16 * 1024 * 1024
STATE_LIMIT = 60 * 1024 * 1024

SCALARS = pl.BlockSpec(memory_space=pltpu.SMEM)
WHOLE = pl.BlockSpec(memory_space=pltpu.VMEM)
FAR = pl.BlockSpec(memory_space=pltpu.HBM)
LEFT = pl.BlockSpec(memory_space=pl.ANY)


def dot(a, b, ca, cb):
    return lax.dot_general(a, b, (((ca,), (cb,)), ((), ())), preferred_element_type=F32)


def place(info, r):
    return pl.multiple_of((info[0] ^ r) * QUARTER, QUARTER)


def state_kernel(first, heads, info, q, k, v, g, *refs):
    outs, (held, hold, sems) = refs[-PARTS - 3 : -3], refs[-3:]
    groups = [(at, min(STEP, heads - at)) for at in range(0, heads, STEP)]
    copies = []
    for n, (at, wide) in enumerate(groups):
        there = pl.ds((first + at) * HEAD_DIM, wide * HEAD_DIM)
        here = pl.ds(at * HEAD_DIM, wide * HEAD_DIM)
        copies.append(
            [
                pltpu.make_async_copy(ref.at[:, there], held.at[i, :, here], sems.at[n, i])
                for i, ref in enumerate((k, v, q, g))
            ]
        )
        for copy in copies[-1]:
            copy.start()
    for n, (at, wide) in enumerate(groups):
        for half in range(2):
            copies[n][2 * half].wait()
            copies[n][2 * half + 1].wait()
            for h in range(at, at + wide):
                cols = slice(h * HEAD_DIM, (h + 1) * HEAD_DIM)
                hold[half] = dot(held[2 * half, :, cols], held[2 * half + 1, :, cols], 0, 0)
                for r in range(PARTS):
                    outs[r][half, h] = hold[half, pl.ds(place(info, r), QUARTER), :]


def states(info, arrays, first, heads, behind):
    rows = arrays[0].shape[0]
    piece = jax.ShapeDtypeStruct((2, heads, QUARTER, HEAD_DIM), F32)
    return pl.pallas_call(
        functools.partial(state_kernel, first, heads),
        out_shape=[piece] * PARTS,
        in_specs=[SCALARS] + [FAR] * 4 + [LEFT] * len(behind),
        out_specs=[WHOLE] * PARTS,
        scratch_shapes=[
            pltpu.VMEM((4, rows, heads * HEAD_DIM), BF16),
            pltpu.VMEM((2, HEAD_DIM, HEAD_DIM), F32),
            pltpu.SemaphoreType.DMA((-(-heads // STEP), 4)),
        ],
        compiler_params=pltpu.CompilerParams(vmem_limit_bytes=STATE_LIMIT),
    )(info, *arrays, *behind)


def add_kernel(info, a, b, c, d, *refs):
    total, halves = refs[-2:]
    total[...] = (a[...] + b[...]) + (c[...] + d[...])
    halves[...] = total[info[1]]


def block_sum(info, pieces, behind):
    shape = pieces[0].shape
    return pl.pallas_call(
        add_kernel,
        out_shape=[jax.ShapeDtypeStruct(shape, F32), jax.ShapeDtypeStruct(shape[1:], F32)],
        in_specs=[SCALARS] + [WHOLE] * PARTS + [LEFT] * len(behind),
        out_specs=[WHOLE] * 2,
        compiler_params=pltpu.CompilerParams(vmem_limit_bytes=VMEM_LIMIT),
    )(info, *pieces, *behind)


def offer_kernel(info, total, across, *refs):
    out = refs[-1]
    upper = info[2] > 0
    whole = 1 - info[1]
    other = info[1]
    send = jnp.logical_xor(upper, whole == 0)
    out[other] = total[other]
    out[whole] = across[...] + jnp.where(send, total[whole], 0.0)


def offer(info, total, across, behind):
    return pl.pallas_call(
        offer_kernel,
        out_shape=jax.ShapeDtypeStruct(total.shape, F32),
        in_specs=[SCALARS, WHOLE, WHOLE] + [LEFT] * len(behind),
        out_specs=WHOLE,
        compiler_params=pltpu.CompilerParams(vmem_limit_bytes=VMEM_LIMIT),
    )(info, total, across, *behind)


def spread_kernel(pair, info, *refs):
    pieces, given, outs = refs[:PARTS], refs[PARTS : PARTS + 1 + pair], refs[-PARTS:]
    mine, node, upper = info[0], info[1], info[2] > 0
    if pair:
        across, other = given
        late = node > 0
        prefix = jnp.where(late, across[...], 0.0) + jnp.where(late | upper, other[0], 0.0)
        suffix = jnp.where(late, 0.0, across[...]) + jnp.where(late & upper, 0.0, other[1])
    else:
        prefix, suffix = given[0][0], given[0][1]
    for r in range(PARTS):
        before, after = prefix, suffix
        for other in range(PARTS):
            if other != r:
                earlier = (mine ^ other) < (mine ^ r)
                before = before + jnp.where(earlier, pieces[other][0], 0.0)
                after = after + jnp.where(earlier, 0.0, pieces[other][1])
        outs[r][0] = before
        outs[r][1] = after


def spread(info, pieces, given, behind):
    return pl.pallas_call(
        functools.partial(spread_kernel, len(given) > 1),
        out_shape=[jax.ShapeDtypeStruct(pieces[0].shape, F32)] * PARTS,
        in_specs=[SCALARS] + [WHOLE] * (PARTS + len(given)) + [LEFT] * len(behind),
        out_specs=[WHOLE] * PARTS,
        compiler_params=pltpu.CompilerParams(vmem_limit_bytes=VMEM_LIMIT),
    )(info, *pieces, *given, *behind)


def sums_outside(total, node, block, blocks):
    everything = lax.all_gather(total, ("node", "local"))
    everything = everything.reshape(-1, blocks, PARTS, *total.shape)
    everything = lax.dynamic_index_in_dim(everything, lax.axis_index("local") % PARTS, 2, False)
    everything = everything.reshape(-1, *total.shape)
    at = node * blocks + block
    earlier = (jnp.arange(everything.shape[0]) < at)[:, None, None, None]
    later = (jnp.arange(everything.shape[0]) > at)[:, None, None, None]
    prefix = jnp.sum(jnp.where(earlier, everything[:, 0], 0.0), axis=0)
    suffix = jnp.sum(jnp.where(later, everything[:, 1], 0.0), axis=0)
    return jnp.stack([prefix, suffix])


def inner_kernel(first, step, q, k, v, g, *refs):
    att, qg, kg, vg = refs[-4:]
    rows = q.shape[0]
    after = lax.broadcasted_iota(jnp.int32, (rows, rows), 0)
    before = lax.broadcasted_iota(jnp.int32, (rows, rows), 1)
    start = pl.program_id(0) * step
    for h in range(step):
        cols = pl.ds(pl.multiple_of((first + start + h) * HEAD_DIM, HEAD_DIM), HEAD_DIM)
        here = pl.ds(pl.multiple_of((start + h) * HEAD_DIM, HEAD_DIM), HEAD_DIM)
        qh, kh, vh, gh = q[:, cols], k[:, cols], v[:, cols], g[:, cols]
        weights = jnp.where(after >= before, dot(qh, kh, 1, 1), 0.0).astype(BF16)
        grad_weights = jnp.where(after >= before, dot(gh, vh, 1, 1), 0.0).astype(BF16)
        att[:, here] = dot(weights, vh, 1, 0)
        qg[:, here] = dot(grad_weights, kh, 1, 0)
        kg[:, here] = dot(grad_weights, qh, 0, 0)
        vg[:, here] = dot(weights, gh, 0, 0)


def inner(arrays, first, heads, step, behind):
    rows = arrays[0].shape[0]
    return pl.pallas_call(
        functools.partial(inner_kernel, first, step),
        out_shape=[jax.ShapeDtypeStruct((rows, heads * HEAD_DIM), F32)] * 4,
        grid=(heads // step,),
        in_specs=[WHOLE] * 4 + [LEFT] * len(behind),
        out_specs=[WHOLE] * 4,
        compiler_params=pltpu.CompilerParams(vmem_limit_bytes=SMALL_LIMIT),
    )(*arrays, *behind)


def finish_kernel(first, step, factor, info, q, k, v, g, *refs):
    terms, pieces = refs[:4], refs[4 : 4 + PARTS]
    outs, hold = refs[-5:-1], refs[-1]
    start = pl.program_id(0) * step
    for h in range(step):
        cols = pl.ds(pl.multiple_of((first + start + h) * HEAD_DIM, HEAD_DIM), HEAD_DIM)
        here = pl.ds(pl.multiple_of((start + h) * HEAD_DIM, HEAD_DIM), HEAD_DIM)
        for r in range(PARTS):
            at = pl.ds(place(info, r), QUARTER)
            hold[h, 0, at, :] = pieces[r][0, start + h].astype(BF16)
            hold[h, 1, at, :] = pieces[r][1, start + h].astype(BF16)
        prefix, suffix = hold[h, 0], hold[h, 1]
        outer = (
            dot(q[:, cols], prefix, 1, 0),
            dot(g[:, cols], prefix, 1, 1),
            dot(v[:, cols], suffix, 1, 1),
            dot(k[:, cols], suffix, 1, 0),
        )
        for out, term, more in zip(outs, terms, outer):
            out[:, h * HEAD_DIM : (h + 1) * HEAD_DIM] = (factor * (term[:, here] + more)).astype(BF16)


def finish(info, arrays, terms, pieces, outs, first, step, factor, behind):
    rows, width = arrays[0].shape
    heads = pieces[0].shape[1]
    columns = pl.BlockSpec((rows, step * HEAD_DIM), lambda i: (0, first // step + i))
    fixed = 1 + 4 + 4 + PARTS
    return pl.pallas_call(
        functools.partial(finish_kernel, first, step, factor),
        out_shape=[jax.ShapeDtypeStruct((rows, width), BF16)] * 4,
        grid=(heads // step,),
        in_specs=[SCALARS] + [WHOLE] * (8 + PARTS) + [LEFT] * (len(outs) + len(behind)),
        out_specs=[columns] * 4,
        scratch_shapes=[pltpu.VMEM((step, 2, HEAD_DIM, HEAD_DIM), BF16)],
        input_output_aliases={fixed + i: i for i in range(len(outs))},
        compiler_params=pltpu.CompilerParams(vmem_limit_bytes=SMALL_LIMIT),
    )(info, *arrays, *terms, *pieces, *outs, *behind)


def swap(array, size, mask):
    return lax.ppermute(array, "local", [(i, i ^ mask) for i in range(size)])


def local(query_rows, key_rows, value_rows, out_grad):
    arrays = (query_rows, key_rows, value_rows, out_grad)
    rows, width = query_rows.shape
    heads = width // HEAD_DIM
    size, nodes = lax.axis_size("local"), lax.axis_size("node")
    blocks = size // PARTS
    assert nodes == 2 and size % PARTS == 0 and sum(CHUNKS) == heads
    factor = 1.0 / math.sqrt(HEAD_DIM * rows * nodes * size)
    node, place_in = lax.axis_index("node"), lax.axis_index("local")
    info = jnp.stack([place_in % PARTS, node, place_in // PARTS]).astype(jnp.int32)

    firsts = [sum(CHUNKS[:i]) for i in range(len(CHUNKS))]
    pieces, given, ready, state, terms = {}, {}, {}, {}, {}
    outs = ()
    last = info
    for stage, i in ORDER:
        first, count = firsts[i], CHUNKS[i]
        behind = [last]
        if stage == "state":
            own = states(info, arrays, first, count, behind)
            last = own[0]
            got = {r: swap(own[r], size, r) for r in (1, 3, 2)}
            pieces[i] = [own[0], got[1], got[2], got[3]]
        elif stage == "sum":
            last, halves = block_sum(info, pieces[i], behind)
            across = lax.ppermute(halves, "node", [(0, 1), (1, 0)])
            state[i] = last, across
        elif stage == "offer":
            total, across = state[i]
            if blocks == 2:
                last = offer(info, total, across, behind)
                given[i] = [across, swap(last, size, PARTS)]
            else:
                given[i] = [sums_outside(total, node, place_in // PARTS, blocks)]
        elif stage == "spread":
            own = spread(info, pieces[i], given[i], behind)
            last = own[0]
            got = {r: swap(own[r], size, r) for r in (1, 3, 2)}
            ready[i] = [own[0], got[1], got[2], got[3]]
        elif stage == "inner":
            terms[i] = inner(arrays, first, count, FINISH_STEP[i], behind)
            last = terms[i][0]
        else:
            outs = finish(
                info, arrays, terms[i], ready[i], outs, first, FINISH_STEP[i], factor, behind
            )
    return tuple(outs)


def solution(mesh):
    rows = P(("group", "node", "local"), None)
    return jax.shard_map(
        local, mesh=mesh, in_specs=(rows,) * 4, out_specs=(rows,) * 4, check_vma=False
    )
```

```python
import functools
import math

import jax
import jax.numpy as jnp
from jax import lax
from jax.experimental import pallas as pl
from jax.experimental.pallas import tpu as pltpu
from jax.sharding import PartitionSpec as P

HEAD_DIM = 128
PARTS = 4
QUARTER = HEAD_DIM // PARTS
CHUNKS = (8, 8)
STEP = 8
TURN = (0, 3, 2, 1)
FINISH_STEP = (4, 4)
ORDER = (
    ("state", 0),
    ("state", 1),
    ("inner", 0),
    ("sum", 0),
    ("offer", 0),
    ("inner", 1),
    ("sum", 1),
    ("offer", 1),
    ("spread", 0),
    ("spread", 1),
    ("finish", 0),
    ("finish", 1),
)

F32 = jnp.float32
BF16 = jnp.bfloat16
VMEM_LIMIT = 40 * 1024 * 1024
SMALL_LIMIT = 16 * 1024 * 1024
STATE_LIMIT = 60 * 1024 * 1024

SCALARS = pl.BlockSpec(memory_space=pltpu.SMEM)
WHOLE = pl.BlockSpec(memory_space=pltpu.VMEM)
FAR = pl.BlockSpec(memory_space=pltpu.HBM)
LEFT = pl.BlockSpec(memory_space=pl.ANY)


def dot(a, b, ca, cb):
    return lax.dot_general(a, b, (((ca,), (cb,)), ((), ())), preferred_element_type=F32)


def place(info, r):
    return pl.multiple_of((info[0] ^ r) * QUARTER, QUARTER)


def state_kernel(first, heads, info, q, k, v, g, *refs):
    outs, (held, hold, sems) = refs[-PARTS - 3 : -3], refs[-3:]
    groups = [(at, min(STEP, heads - at)) for at in range(0, heads, STEP)]
    copies = []
    for n, (at, wide) in enumerate(groups):
        there = pl.ds((first + at) * HEAD_DIM, wide * HEAD_DIM)
        here = pl.ds(at * HEAD_DIM, wide * HEAD_DIM)
        copies.append(
            [
                pltpu.make_async_copy(ref.at[:, there], held.at[i, :, here], sems.at[n, i])
                for i, ref in enumerate((k, v, q, g))
            ]
        )
        for copy in copies[-1]:
            copy.start()
    for n, (at, wide) in enumerate(groups):
        for half in range(2):
            copies[n][2 * half].wait()
            copies[n][2 * half + 1].wait()
            for h in range(at, at + wide):
                cols = slice(h * HEAD_DIM, (h + 1) * HEAD_DIM)
                hold[half] = dot(held[2 * half, :, cols], held[2 * half + 1, :, cols], 0, 0)
                for r in range(PARTS):
                    outs[r][half, h] = hold[half, pl.ds(place(info, r), QUARTER), :]


def states(info, arrays, first, heads, behind):
    rows = arrays[0].shape[0]
    piece = jax.ShapeDtypeStruct((2, heads, QUARTER, HEAD_DIM), F32)
    return pl.pallas_call(
        functools.partial(state_kernel, first, heads),
        out_shape=[piece] * PARTS,
        in_specs=[SCALARS] + [FAR] * 4 + [LEFT] * len(behind),
        out_specs=[WHOLE] * PARTS,
        scratch_shapes=[
            pltpu.VMEM((4, rows, heads * HEAD_DIM), BF16),
            pltpu.VMEM((2, HEAD_DIM, HEAD_DIM), F32),
            pltpu.SemaphoreType.DMA((-(-heads // STEP), 4)),
        ],
        compiler_params=pltpu.CompilerParams(vmem_limit_bytes=STATE_LIMIT),
    )(info, *arrays, *behind)


def add_kernel(info, a, b, c, d, *refs):
    total, halves = refs[-2:]
    total[...] = (a[...] + b[...]) + (c[...] + d[...])
    halves[...] = total[info[1]]


def block_sum(info, pieces, behind):
    shape = pieces[0].shape
    return pl.pallas_call(
        add_kernel,
        out_shape=[jax.ShapeDtypeStruct(shape, F32), jax.ShapeDtypeStruct(shape[1:], F32)],
        in_specs=[SCALARS] + [WHOLE] * PARTS + [LEFT] * len(behind),
        out_specs=[WHOLE] * 2,
        compiler_params=pltpu.CompilerParams(vmem_limit_bytes=VMEM_LIMIT),
    )(info, *pieces, *behind)


def offer_kernel(info, total, across, *refs):
    out = refs[-1]
    upper = info[2] > 0
    whole = 1 - info[1]
    other = info[1]
    send = jnp.logical_xor(upper, whole == 0)
    out[other] = total[other]
    out[whole] = across[...] + jnp.where(send, total[whole], 0.0)


def offer(info, total, across, behind):
    return pl.pallas_call(
        offer_kernel,
        out_shape=jax.ShapeDtypeStruct(total.shape, F32),
        in_specs=[SCALARS, WHOLE, WHOLE] + [LEFT] * len(behind),
        out_specs=WHOLE,
        compiler_params=pltpu.CompilerParams(vmem_limit_bytes=VMEM_LIMIT),
    )(info, total, across, *behind)


def spread_kernel(pair, info, *refs):
    pieces, given, outs = refs[:PARTS], refs[PARTS : PARTS + 1 + pair], refs[-PARTS:]
    mine, node, upper = info[0], info[1], info[2] > 0
    if pair:
        across, other = given
        late = node > 0
        prefix = jnp.where(late, across[...], 0.0) + jnp.where(late | upper, other[0], 0.0)
        suffix = jnp.where(late, 0.0, across[...]) + jnp.where(late & upper, 0.0, other[1])
    else:
        prefix, suffix = given[0][0], given[0][1]
    for r in range(PARTS):
        before, after = prefix, suffix
        for other in range(PARTS):
            if other != r:
                earlier = (mine ^ other) < (mine ^ r)
                before = before + jnp.where(earlier, pieces[other][0], 0.0)
                after = after + jnp.where(earlier, 0.0, pieces[other][1])
        outs[r][0] = before
        outs[r][1] = after


def spread(info, pieces, given, behind):
    return pl.pallas_call(
        functools.partial(spread_kernel, len(given) > 1),
        out_shape=[jax.ShapeDtypeStruct(pieces[0].shape, F32)] * PARTS,
        in_specs=[SCALARS] + [WHOLE] * (PARTS + len(given)) + [LEFT] * len(behind),
        out_specs=[WHOLE] * PARTS,
        compiler_params=pltpu.CompilerParams(vmem_limit_bytes=VMEM_LIMIT),
    )(info, *pieces, *given, *behind)


def sums_outside(total, node, block, blocks):
    everything = lax.all_gather(total, ("node", "local"))
    everything = everything.reshape(-1, blocks, PARTS, *total.shape)
    everything = lax.dynamic_index_in_dim(everything, lax.axis_index("local") % PARTS, 2, False)
    everything = everything.reshape(-1, *total.shape)
    at = node * blocks + block
    earlier = (jnp.arange(everything.shape[0]) < at)[:, None, None, None]
    later = (jnp.arange(everything.shape[0]) > at)[:, None, None, None]
    prefix = jnp.sum(jnp.where(earlier, everything[:, 0], 0.0), axis=0)
    suffix = jnp.sum(jnp.where(later, everything[:, 1], 0.0), axis=0)
    return jnp.stack([prefix, suffix])


def inner_kernel(first, step, q, k, v, g, *refs):
    att, qg, kg, vg = refs[-4:]
    rows = q.shape[0]
    after = lax.broadcasted_iota(jnp.int32, (rows, rows), 0)
    before = lax.broadcasted_iota(jnp.int32, (rows, rows), 1)
    start = pl.program_id(0) * step
    for h in range(step):
        cols = pl.ds(pl.multiple_of((first + start + h) * HEAD_DIM, HEAD_DIM), HEAD_DIM)
        here = pl.ds(pl.multiple_of((start + h) * HEAD_DIM, HEAD_DIM), HEAD_DIM)
        qh, kh, vh, gh = q[:, cols], k[:, cols], v[:, cols], g[:, cols]
        weights = jnp.where(after >= before, dot(qh, kh, 1, 1), 0.0).astype(BF16)
        grad_weights = jnp.where(after >= before, dot(gh, vh, 1, 1), 0.0).astype(BF16)
        att[:, here] = dot(weights, vh, 1, 0)
        qg[:, here] = dot(grad_weights, kh, 1, 0)
        kg[:, here] = dot(grad_weights, qh, 0, 0)
        vg[:, here] = dot(weights, gh, 0, 0)


def inner(arrays, first, heads, step, behind):
    rows = arrays[0].shape[0]
    return pl.pallas_call(
        functools.partial(inner_kernel, first, step),
        out_shape=[jax.ShapeDtypeStruct((rows, heads * HEAD_DIM), F32)] * 4,
        grid=(heads // step,),
        in_specs=[WHOLE] * 4 + [LEFT] * len(behind),
        out_specs=[WHOLE] * 4,
        compiler_params=pltpu.CompilerParams(vmem_limit_bytes=SMALL_LIMIT),
    )(*arrays, *behind)


def finish_kernel(first, step, factor, info, q, k, v, g, *refs):
    terms, pieces = refs[:4], refs[4 : 4 + PARTS]
    outs, hold = refs[-5:-1], refs[-1]
    start = pl.program_id(0) * step
    for h in range(step):
        cols = pl.ds(pl.multiple_of((first + start + h) * HEAD_DIM, HEAD_DIM), HEAD_DIM)
        here = pl.ds(pl.multiple_of((start + h) * HEAD_DIM, HEAD_DIM), HEAD_DIM)
        for r, piece in zip(TURN, pieces):
            at = pl.ds(place(info, r), QUARTER)
            hold[h, 0, at, :] = piece[0, start + h].astype(BF16)
            hold[h, 1, at, :] = piece[1, start + h].astype(BF16)
        prefix, suffix = hold[h, 0], hold[h, 1]
        outer = (
            dot(q[:, cols], prefix, 1, 0),
            dot(g[:, cols], prefix, 1, 1),
            dot(v[:, cols], suffix, 1, 1),
            dot(k[:, cols], suffix, 1, 0),
        )
        for out, term, more in zip(outs, terms, outer):
            out[:, h * HEAD_DIM : (h + 1) * HEAD_DIM] = (factor * (term[:, here] + more)).astype(BF16)


def finish(info, arrays, terms, pieces, outs, first, step, factor, behind):
    rows, width = arrays[0].shape
    heads = pieces[0].shape[1]
    columns = pl.BlockSpec((rows, step * HEAD_DIM), lambda i: (0, first // step + i))
    fixed = 1 + 4 + 4 + PARTS
    return pl.pallas_call(
        functools.partial(finish_kernel, first, step, factor),
        out_shape=[jax.ShapeDtypeStruct((rows, width), BF16)] * 4,
        grid=(heads // step,),
        in_specs=[SCALARS] + [WHOLE] * (8 + PARTS) + [LEFT] * (len(outs) + len(behind)),
        out_specs=[columns] * 4,
        scratch_shapes=[pltpu.VMEM((step, 2, HEAD_DIM, HEAD_DIM), BF16)],
        input_output_aliases={fixed + i: i for i in range(len(outs))},
        compiler_params=pltpu.CompilerParams(vmem_limit_bytes=SMALL_LIMIT),
    )(info, *arrays, *terms, *pieces, *outs, *behind)


def swap(array, size, mask):
    return lax.ppermute(array, "local", [(i, i ^ mask) for i in range(size)])


def local(query_rows, key_rows, value_rows, out_grad):
    arrays = (query_rows, key_rows, value_rows, out_grad)
    rows, width = query_rows.shape
    heads = width // HEAD_DIM
    size, nodes = lax.axis_size("local"), lax.axis_size("node")
    blocks = size // PARTS
    assert nodes == 2 and size % PARTS == 0 and sum(CHUNKS) == heads
    factor = 1.0 / math.sqrt(HEAD_DIM * rows * nodes * size)
    node, place_in = lax.axis_index("node"), lax.axis_index("local")
    info = jnp.stack([place_in % PARTS, node, place_in // PARTS]).astype(jnp.int32)

    firsts = [sum(CHUNKS[:i]) for i in range(len(CHUNKS))]
    pieces, given, ready, state, terms = {}, {}, {}, {}, {}
    outs = ()
    last = info
    for stage, i in ORDER:
        first, count = firsts[i], CHUNKS[i]
        behind = [last]
        if stage == "state":
            own = states(info, arrays, first, count, behind)
            last = own[0]
            got = {r: swap(own[r], size, r) for r in TURN[1:]}
            pieces[i] = [own[0], got[1], got[2], got[3]]
        elif stage == "sum":
            last, halves = block_sum(info, [pieces[i][r] for r in TURN], behind)
            across = lax.ppermute(halves, "node", [(0, 1), (1, 0)])
            state[i] = last, across
        elif stage == "offer":
            total, across = state[i]
            if blocks == 2:
                last = offer(info, total, across, behind)
                given[i] = [across, swap(last, size, PARTS)]
            else:
                given[i] = [sums_outside(total, node, place_in // PARTS, blocks)]
        elif stage == "spread":
            own = spread(info, pieces[i], given[i], behind)
            last = own[0]
            got = {r: swap(own[r], size, r) for r in TURN[1:]}
            ready[i] = [own[0], got[1], got[2], got[3]]
        elif stage == "inner":
            terms[i] = inner(arrays, first, count, FINISH_STEP[i], behind)
            last = terms[i][0]
        else:
            outs = finish(
                info, arrays, terms[i], [ready[i][r] for r in TURN], outs, first, FINISH_STEP[i], factor, behind
            )
    return tuple(outs)


def solution(mesh):
    rows = P(("group", "node", "local"), None)
    return jax.shard_map(
        local, mesh=mesh, in_specs=(rows,) * 4, out_specs=(rows,) * 4, check_vma=False
    )
```

```python
import functools
import math

import jax
import jax.numpy as jnp
from jax import lax
from jax.experimental import pallas as pl
from jax.experimental.pallas import tpu as pltpu
from jax.sharding import PartitionSpec as P

HEAD_DIM = 128
PARTS = 4
QUARTER = HEAD_DIM // PARTS
CHUNKS = (8, 8)
STEP = 8
TURN = (0, 3, 2, 1)
FINISH_STEP = (4, 4)
ORDER = (
    ("state", 0),
    ("state", 1),
    ("inner", 0),
    ("sum", 0),
    ("offer", 0),
    ("inner", 1),
    ("sum", 1),
    ("offer", 1),
    ("spread", 0),
    ("spread", 1),
    ("finish", 0),
    ("finish", 1),
)

F32 = jnp.float32
BF16 = jnp.bfloat16
VMEM_LIMIT = 40 * 1024 * 1024
SMALL_LIMIT = 16 * 1024 * 1024
STATE_LIMIT = 60 * 1024 * 1024

SCALARS = pl.BlockSpec(memory_space=pltpu.SMEM)
WHOLE = pl.BlockSpec(memory_space=pltpu.VMEM)
FAR = pl.BlockSpec(memory_space=pltpu.HBM)
LEFT = pl.BlockSpec(memory_space=pl.ANY)


def dot(a, b, ca, cb):
    return lax.dot_general(a, b, (((ca,), (cb,)), ((), ())), preferred_element_type=F32)


def place(info, r):
    return pl.multiple_of((info[0] ^ r) * QUARTER, QUARTER)


def state_kernel(first, heads, info, q, k, v, g, *refs):
    outs, (held, hold, sems) = refs[-PARTS - 3 : -3], refs[-3:]
    groups = [(at, min(STEP, heads - at)) for at in range(0, heads, STEP)]
    copies = []
    for n, (at, wide) in enumerate(groups):
        there = pl.ds((first + at) * HEAD_DIM, wide * HEAD_DIM)
        here = pl.ds(at * HEAD_DIM, wide * HEAD_DIM)
        copies.append(
            [
                pltpu.make_async_copy(ref.at[:, there], held.at[i, :, here], sems.at[n, i])
                for i, ref in enumerate((k, v, q, g))
            ]
        )
        for copy in copies[-1]:
            copy.start()
    for n, (at, wide) in enumerate(groups):
        for half in range(2):
            copies[n][2 * half].wait()
            copies[n][2 * half + 1].wait()
            for h in range(at, at + wide):
                cols = slice(h * HEAD_DIM, (h + 1) * HEAD_DIM)
                hold[half] = dot(held[2 * half, :, cols], held[2 * half + 1, :, cols], 0, 0)
                for r in range(PARTS):
                    outs[r][half, h] = hold[half, pl.ds(place(info, r), QUARTER), :]


def states(info, arrays, first, heads, behind):
    rows = arrays[0].shape[0]
    piece = jax.ShapeDtypeStruct((2, heads, QUARTER, HEAD_DIM), F32)
    return pl.pallas_call(
        functools.partial(state_kernel, first, heads),
        out_shape=[piece] * PARTS,
        in_specs=[SCALARS] + [FAR] * 4 + [LEFT] * len(behind),
        out_specs=[WHOLE] * PARTS,
        scratch_shapes=[
            pltpu.VMEM((4, rows, heads * HEAD_DIM), BF16),
            pltpu.VMEM((2, HEAD_DIM, HEAD_DIM), F32),
            pltpu.SemaphoreType.DMA((-(-heads // STEP), 4)),
        ],
        compiler_params=pltpu.CompilerParams(vmem_limit_bytes=STATE_LIMIT),
    )(info, *arrays, *behind)


def add_kernel(info, a, b, c, d, *refs):
    total, halves = refs[-2:]
    total[...] = (a[...] + b[...]) + (c[...] + d[...])
    halves[...] = total[info[1]]


def block_sum(info, pieces, behind):
    shape = pieces[0].shape
    return pl.pallas_call(
        add_kernel,
        out_shape=[jax.ShapeDtypeStruct(shape, F32), jax.ShapeDtypeStruct(shape[1:], F32)],
        in_specs=[SCALARS] + [WHOLE] * PARTS + [LEFT] * len(behind),
        out_specs=[WHOLE] * 2,
        compiler_params=pltpu.CompilerParams(vmem_limit_bytes=VMEM_LIMIT),
    )(info, *pieces, *behind)


def offer_kernel(info, total, across, *refs):
    out = refs[-1]
    node, upper = info[1], jnp.where(info[2] > 0, 1, 0)
    half = out.shape[1]
    for j in range(2):
        heads = slice(j * half, (j + 1) * half)
        out[j] = total[upper, heads] + jnp.where(node != upper, across[heads], 0.0)
    heads = pl.ds(node * half, half)
    out[2] = jnp.where(node == upper, across[heads], total[1 - upper, heads])


def offer(info, total, across, behind):
    heads = total.shape[1]
    return pl.pallas_call(
        offer_kernel,
        out_shape=jax.ShapeDtypeStruct((3, heads // 2, *total.shape[2:]), F32),
        in_specs=[SCALARS, WHOLE, WHOLE] + [LEFT] * len(behind),
        out_specs=WHOLE,
        compiler_params=pltpu.CompilerParams(vmem_limit_bytes=VMEM_LIMIT),
    )(info, total, across, *behind)


def spread_kernel(pair, info, *refs):
    count = 3 if pair else 1
    pieces, given, outs = refs[:PARTS], refs[PARTS : PARTS + count], refs[-PARTS:]
    mine, node, upper = info[0], info[1], jnp.where(info[2] > 0, 1, 0)
    half = pieces[0].shape[1] // 2
    for j in range(2):
        heads = slice(j * half, (j + 1) * half)
        if pair:
            across, here, there = given
            alone = node != upper
            main = here[j]
            extra = jnp.where(node == j, here[2], there[2])
            whole = across[heads] + jnp.where(alone, extra, main)
            part = jnp.where(alone, main, 0.0)
            prefix = jnp.where(node > 0, whole, part)
            suffix = jnp.where(node > 0, part, whole)
        else:
            prefix, suffix = given[0][0, heads], given[0][1, heads]
        for r in range(PARTS):
            before, after = prefix, suffix
            for other in range(PARTS):
                if other != r:
                    earlier = (mine ^ other) < (mine ^ r)
                    before = before + jnp.where(earlier, pieces[other][0, heads], 0.0)
                    after = after + jnp.where(earlier, 0.0, pieces[other][1, heads])
            outs[r][0, heads] = before
            outs[r][1, heads] = after


def spread(info, pieces, given, behind):
    return pl.pallas_call(
        functools.partial(spread_kernel, len(given) > 1),
        out_shape=[jax.ShapeDtypeStruct(pieces[0].shape, F32)] * PARTS,
        in_specs=[SCALARS] + [WHOLE] * (PARTS + len(given)) + [LEFT] * len(behind),
        out_specs=[WHOLE] * PARTS,
        compiler_params=pltpu.CompilerParams(vmem_limit_bytes=VMEM_LIMIT),
    )(info, *pieces, *given, *behind)


def sums_outside(total, node, block, blocks):
    everything = lax.all_gather(total, ("node", "local"))
    everything = everything.reshape(-1, blocks, PARTS, *total.shape)
    everything = lax.dynamic_index_in_dim(everything, lax.axis_index("local") % PARTS, 2, False)
    everything = everything.reshape(-1, *total.shape)
    at = node * blocks + block
    earlier = (jnp.arange(everything.shape[0]) < at)[:, None, None, None]
    later = (jnp.arange(everything.shape[0]) > at)[:, None, None, None]
    prefix = jnp.sum(jnp.where(earlier, everything[:, 0], 0.0), axis=0)
    suffix = jnp.sum(jnp.where(later, everything[:, 1], 0.0), axis=0)
    return jnp.stack([prefix, suffix])


def inner_kernel(first, step, q, k, v, g, *refs):
    att, qg, kg, vg = refs[-4:]
    rows = q.shape[0]
    after = lax.broadcasted_iota(jnp.int32, (rows, rows), 0)
    before = lax.broadcasted_iota(jnp.int32, (rows, rows), 1)
    start = pl.program_id(0) * step
    for h in range(step):
        cols = pl.ds(pl.multiple_of((first + start + h) * HEAD_DIM, HEAD_DIM), HEAD_DIM)
        here = pl.ds(pl.multiple_of((start + h) * HEAD_DIM, HEAD_DIM), HEAD_DIM)
        qh, kh, vh, gh = q[:, cols], k[:, cols], v[:, cols], g[:, cols]
        weights = jnp.where(after >= before, dot(qh, kh, 1, 1), 0.0).astype(BF16)
        grad_weights = jnp.where(after >= before, dot(gh, vh, 1, 1), 0.0).astype(BF16)
        att[:, here] = dot(weights, vh, 1, 0)
        qg[:, here] = dot(grad_weights, kh, 1, 0)
        kg[:, here] = dot(grad_weights, qh, 0, 0)
        vg[:, here] = dot(weights, gh, 0, 0)


def inner(arrays, first, heads, step, behind):
    rows = arrays[0].shape[0]
    return pl.pallas_call(
        functools.partial(inner_kernel, first, step),
        out_shape=[jax.ShapeDtypeStruct((rows, heads * HEAD_DIM), F32)] * 4,
        grid=(heads // step,),
        in_specs=[WHOLE] * 4 + [LEFT] * len(behind),
        out_specs=[WHOLE] * 4,
        compiler_params=pltpu.CompilerParams(vmem_limit_bytes=SMALL_LIMIT),
    )(*arrays, *behind)


def finish_kernel(first, step, factor, info, q, k, v, g, *refs):
    terms, pieces = refs[:4], refs[4 : 4 + PARTS]
    outs, hold = refs[-5:-1], refs[-1]
    start = pl.program_id(0) * step
    for h in range(step):
        cols = pl.ds(pl.multiple_of((first + start + h) * HEAD_DIM, HEAD_DIM), HEAD_DIM)
        here = pl.ds(pl.multiple_of((start + h) * HEAD_DIM, HEAD_DIM), HEAD_DIM)
        for r, piece in zip(TURN, pieces):
            at = pl.ds(place(info, r), QUARTER)
            hold[h, 0, at, :] = piece[0, start + h].astype(BF16)
            hold[h, 1, at, :] = piece[1, start + h].astype(BF16)
        prefix, suffix = hold[h, 0], hold[h, 1]
        outer = (
            dot(q[:, cols], prefix, 1, 0),
            dot(g[:, cols], prefix, 1, 1),
            dot(v[:, cols], suffix, 1, 1),
            dot(k[:, cols], suffix, 1, 0),
        )
        for out, term, more in zip(outs, terms, outer):
            out[:, h * HEAD_DIM : (h + 1) * HEAD_DIM] = (factor * (term[:, here] + more)).astype(BF16)


def finish(info, arrays, terms, pieces, outs, first, step, factor, behind):
    rows, width = arrays[0].shape
    heads = pieces[0].shape[1]
    columns = pl.BlockSpec((rows, step * HEAD_DIM), lambda i: (0, first // step + i))
    fixed = 1 + 4 + 4 + PARTS
    return pl.pallas_call(
        functools.partial(finish_kernel, first, step, factor),
        out_shape=[jax.ShapeDtypeStruct((rows, width), BF16)] * 4,
        grid=(heads // step,),
        in_specs=[SCALARS] + [WHOLE] * (8 + PARTS) + [LEFT] * (len(outs) + len(behind)),
        out_specs=[columns] * 4,
        scratch_shapes=[pltpu.VMEM((step, 2, HEAD_DIM, HEAD_DIM), BF16)],
        input_output_aliases={fixed + i: i for i in range(len(outs))},
        compiler_params=pltpu.CompilerParams(vmem_limit_bytes=SMALL_LIMIT),
    )(info, *arrays, *terms, *pieces, *outs, *behind)


def swap(array, size, mask):
    return lax.ppermute(array, "local", [(i, i ^ mask) for i in range(size)])


def local(query_rows, key_rows, value_rows, out_grad):
    arrays = (query_rows, key_rows, value_rows, out_grad)
    rows, width = query_rows.shape
    heads = width // HEAD_DIM
    size, nodes = lax.axis_size("local"), lax.axis_size("node")
    blocks = size // PARTS
    assert nodes == 2 and size % PARTS == 0 and sum(CHUNKS) == heads
    factor = 1.0 / math.sqrt(HEAD_DIM * rows * nodes * size)
    node, place_in = lax.axis_index("node"), lax.axis_index("local")
    info = jnp.stack([place_in % PARTS, node, place_in // PARTS]).astype(jnp.int32)

    firsts = [sum(CHUNKS[:i]) for i in range(len(CHUNKS))]
    pieces, given, ready, state, terms = {}, {}, {}, {}, {}
    outs = ()
    last = info
    for stage, i in ORDER:
        first, count = firsts[i], CHUNKS[i]
        behind = [last]
        if stage == "state":
            own = states(info, arrays, first, count, behind)
            last = own[0]
            got = {r: swap(own[r], size, r) for r in TURN[1:]}
            pieces[i] = [own[0], got[1], got[2], got[3]]
        elif stage == "sum":
            last, halves = block_sum(info, [pieces[i][r] for r in TURN], behind)
            across = lax.ppermute(halves, "node", [(0, 1), (1, 0)])
            state[i] = last, across
        elif stage == "offer":
            total, across = state[i]
            if blocks == 2:
                last = offer(info, total, across, behind)
                other = swap(last, size, PARTS)
                given[i] = [across, other, lax.ppermute(other, "node", [(0, 1), (1, 0)])]
            else:
                given[i] = [sums_outside(total, node, place_in // PARTS, blocks)]
        elif stage == "spread":
            own = spread(info, pieces[i], given[i], behind)
            last = own[0]
            got = {r: swap(own[r], size, r) for r in TURN[1:]}
            ready[i] = [own[0], got[1], got[2], got[3]]
        elif stage == "inner":
            terms[i] = inner(arrays, first, count, FINISH_STEP[i], behind)
            last = terms[i][0]
        else:
            outs = finish(
                info, arrays, terms[i], [ready[i][r] for r in TURN], outs, first, FINISH_STEP[i], factor, behind
            )
    return tuple(outs)


def solution(mesh):
    rows = P(("group", "node", "local"), None)
    return jax.shard_map(
        local, mesh=mesh, in_specs=(rows,) * 4, out_specs=(rows,) * 4, check_vma=False
    )
```

```python
import functools
import math

import jax
import jax.numpy as jnp
from jax import lax
from jax.experimental import pallas as pl
from jax.experimental.pallas import tpu as pltpu
from jax.sharding import PartitionSpec as P

HEAD_DIM = 128
PARTS = 4
QUARTER = HEAD_DIM // PARTS
CHUNKS = (8, 8)
STEP = 8
TURN = (0, 3, 2, 1)
TURN_BACK = (0, 3, 2, 1)
FINISH_STEP = (4, 4)
ORDER = (
    ("state", 0),
    ("state", 1),
    ("inner", 0),
    ("sum", 0),
    ("offer", 0),
    ("inner", 1),
    ("sum", 1),
    ("offer", 1),
    ("spread", 0),
    ("spread", 1),
    ("finish", 0),
    ("finish", 1),
)

F32 = jnp.float32
BF16 = jnp.bfloat16
VMEM_LIMIT = 40 * 1024 * 1024
SMALL_LIMIT = 16 * 1024 * 1024
STATE_LIMIT = 60 * 1024 * 1024

SCALARS = pl.BlockSpec(memory_space=pltpu.SMEM)
WHOLE = pl.BlockSpec(memory_space=pltpu.VMEM)
FAR = pl.BlockSpec(memory_space=pltpu.HBM)
LEFT = pl.BlockSpec(memory_space=pl.ANY)


def dot(a, b, ca, cb):
    return lax.dot_general(a, b, (((ca,), (cb,)), ((), ())), preferred_element_type=F32)


def unpack(info):
    return (info[0] >> 1) % PARTS, info[0] & 1, (info[0] >> 1) // PARTS


def place(info, r):
    return pl.multiple_of((info[0] ^ r) * QUARTER, QUARTER)


def state_kernel(first, heads, info, q, k, v, g, *refs):
    info = unpack(info)
    outs, (held, hold, sems) = refs[-PARTS - 3 : -3], refs[-3:]
    groups = [(at, min(STEP, heads - at)) for at in range(0, heads, STEP)]
    copies = []
    for n, (at, wide) in enumerate(groups):
        there = pl.ds((first + at) * HEAD_DIM, wide * HEAD_DIM)
        here = pl.ds(at * HEAD_DIM, wide * HEAD_DIM)
        copies.append(
            [
                pltpu.make_async_copy(ref.at[:, there], held.at[i, :, here], sems.at[n, i])
                for i, ref in enumerate((k, v, q, g))
            ]
        )
        for copy in copies[-1]:
            copy.start()
    for n, (at, wide) in enumerate(groups):
        for half in range(2):
            copies[n][2 * half].wait()
            copies[n][2 * half + 1].wait()
            for h in range(at, at + wide):
                cols = slice(h * HEAD_DIM, (h + 1) * HEAD_DIM)
                hold[half] = dot(held[2 * half, :, cols], held[2 * half + 1, :, cols], 0, 0)
                for r in range(PARTS):
                    outs[r][half, h] = hold[half, pl.ds(place(info, r), QUARTER), :]


def states(info, arrays, first, heads, behind):
    rows = arrays[0].shape[0]
    piece = jax.ShapeDtypeStruct((2, heads, QUARTER, HEAD_DIM), F32)
    return pl.pallas_call(
        functools.partial(state_kernel, first, heads),
        out_shape=[piece] * PARTS,
        in_specs=[SCALARS] + [FAR] * 4 + [LEFT] * len(behind),
        out_specs=[WHOLE] * PARTS,
        scratch_shapes=[
            pltpu.VMEM((4, rows, heads * HEAD_DIM), BF16),
            pltpu.VMEM((2, HEAD_DIM, HEAD_DIM), F32),
            pltpu.SemaphoreType.DMA((-(-heads // STEP), 4)),
        ],
        compiler_params=pltpu.CompilerParams(vmem_limit_bytes=STATE_LIMIT),
    )(info, *arrays, *behind)


def add_kernel(info, a, b, c, d, *refs):
    info = unpack(info)
    total, halves = refs[-2:]
    total[...] = (a[...] + b[...]) + (c[...] + d[...])
    halves[...] = total[info[1]]


def block_sum(info, pieces, behind):
    shape = pieces[0].shape
    return pl.pallas_call(
        add_kernel,
        out_shape=[jax.ShapeDtypeStruct(shape, F32), jax.ShapeDtypeStruct(shape[1:], F32)],
        in_specs=[SCALARS] + [WHOLE] * PARTS + [LEFT] * len(behind),
        out_specs=[WHOLE] * 2,
        compiler_params=pltpu.CompilerParams(vmem_limit_bytes=VMEM_LIMIT),
    )(info, *pieces, *behind)


def offer_kernel(info, total, across, *refs):
    info = unpack(info)
    out = refs[-1]
    node, upper = info[1], jnp.where(info[2] > 0, 1, 0)
    half = out.shape[1]
    for j in range(2):
        heads = slice(j * half, (j + 1) * half)
        out[j] = total[upper, heads] + jnp.where(node != upper, across[heads], 0.0)
    heads = pl.ds(node * half, half)
    out[2] = jnp.where(node == upper, across[heads], total[1 - upper, heads])


def offer(info, total, across, behind):
    heads = total.shape[1]
    return pl.pallas_call(
        offer_kernel,
        out_shape=jax.ShapeDtypeStruct((3, heads // 2, *total.shape[2:]), F32),
        in_specs=[SCALARS, WHOLE, WHOLE] + [LEFT] * len(behind),
        out_specs=WHOLE,
        compiler_params=pltpu.CompilerParams(vmem_limit_bytes=VMEM_LIMIT),
    )(info, total, across, *behind)


def spread_kernel(pair, info, *refs):
    info = unpack(info)
    count = 3 if pair else 1
    pieces, given, outs = refs[:PARTS], refs[PARTS : PARTS + count], refs[-PARTS:]
    mine, node, upper = info[0], info[1], jnp.where(info[2] > 0, 1, 0)
    half = pieces[0].shape[1] // 2
    for j in range(2):
        heads = slice(j * half, (j + 1) * half)
        if pair:
            across, here, there = given
            alone = node != upper
            main = here[j]
            extra = jnp.where(node == j, here[2], there[2])
            whole = across[heads] + jnp.where(alone, extra, main)
            part = jnp.where(alone, main, 0.0)
            prefix = jnp.where(node > 0, whole, part)
            suffix = jnp.where(node > 0, part, whole)
        else:
            prefix, suffix = given[0][0, heads], given[0][1, heads]
        for r in range(PARTS):
            before, after = prefix, suffix
            for other in range(PARTS):
                if other != r:
                    earlier = (mine ^ other) < (mine ^ r)
                    before = before + jnp.where(earlier, pieces[other][0, heads], 0.0)
                    after = after + jnp.where(earlier, 0.0, pieces[other][1, heads])
            outs[r][0, heads] = before
            outs[r][1, heads] = after


def spread(info, pieces, given, behind):
    return pl.pallas_call(
        functools.partial(spread_kernel, len(given) > 1),
        out_shape=[jax.ShapeDtypeStruct(pieces[0].shape, F32)] * PARTS,
        in_specs=[SCALARS] + [WHOLE] * (PARTS + len(given)) + [LEFT] * len(behind),
        out_specs=[WHOLE] * PARTS,
        compiler_params=pltpu.CompilerParams(vmem_limit_bytes=VMEM_LIMIT),
    )(info, *pieces, *given, *behind)


def sums_outside(total, node, block, blocks):
    everything = lax.all_gather(total, ("node", "local"))
    everything = everything.reshape(-1, blocks, PARTS, *total.shape)
    everything = lax.dynamic_index_in_dim(everything, lax.axis_index("local") % PARTS, 2, False)
    everything = everything.reshape(-1, *total.shape)
    at = node * blocks + block
    earlier = (jnp.arange(everything.shape[0]) < at)[:, None, None, None]
    later = (jnp.arange(everything.shape[0]) > at)[:, None, None, None]
    prefix = jnp.sum(jnp.where(earlier, everything[:, 0], 0.0), axis=0)
    suffix = jnp.sum(jnp.where(later, everything[:, 1], 0.0), axis=0)
    return jnp.stack([prefix, suffix])


def inner_kernel(first, step, q, k, v, g, *refs):
    att, qg, kg, vg = refs[-4:]
    rows = q.shape[0]
    after = lax.broadcasted_iota(jnp.int32, (rows, rows), 0)
    before = lax.broadcasted_iota(jnp.int32, (rows, rows), 1)
    start = pl.program_id(0) * step
    for h in range(step):
        cols = pl.ds(pl.multiple_of((first + start + h) * HEAD_DIM, HEAD_DIM), HEAD_DIM)
        here = pl.ds(pl.multiple_of((start + h) * HEAD_DIM, HEAD_DIM), HEAD_DIM)
        qh, kh, vh, gh = q[:, cols], k[:, cols], v[:, cols], g[:, cols]
        weights = jnp.where(after >= before, dot(qh, kh, 1, 1), 0.0).astype(BF16)
        grad_weights = jnp.where(after >= before, dot(gh, vh, 1, 1), 0.0).astype(BF16)
        att[:, here] = dot(weights, vh, 1, 0)
        qg[:, here] = dot(grad_weights, kh, 1, 0)
        kg[:, here] = dot(grad_weights, qh, 0, 0)
        vg[:, here] = dot(weights, gh, 0, 0)


def inner(arrays, first, heads, step, behind):
    rows = arrays[0].shape[0]
    return pl.pallas_call(
        functools.partial(inner_kernel, first, step),
        out_shape=[jax.ShapeDtypeStruct((rows, heads * HEAD_DIM), F32)] * 4,
        grid=(heads // step,),
        in_specs=[WHOLE] * 4 + [LEFT] * len(behind),
        out_specs=[WHOLE] * 4,
        compiler_params=pltpu.CompilerParams(vmem_limit_bytes=SMALL_LIMIT),
    )(*arrays, *behind)


def finish_kernel(first, step, factor, info, q, k, v, g, *refs):
    info = unpack(info)
    terms, pieces = refs[:4], refs[4 : 4 + PARTS]
    outs, hold = refs[-5:-1], refs[-1]
    start = pl.program_id(0) * step
    for h in range(step):
        cols = pl.ds(pl.multiple_of((first + start + h) * HEAD_DIM, HEAD_DIM), HEAD_DIM)
        here = pl.ds(pl.multiple_of((start + h) * HEAD_DIM, HEAD_DIM), HEAD_DIM)
        for r, piece in zip(TURN_BACK, pieces):
            at = pl.ds(place(info, r), QUARTER)
            hold[h, 0, at, :] = piece[0, start + h].astype(BF16)
            hold[h, 1, at, :] = piece[1, start + h].astype(BF16)
        prefix, suffix = hold[h, 0], hold[h, 1]
        outer = (
            dot(q[:, cols], prefix, 1, 0),
            dot(g[:, cols], prefix, 1, 1),
            dot(v[:, cols], suffix, 1, 1),
            dot(k[:, cols], suffix, 1, 0),
        )
        for out, term, more in zip(outs, terms, outer):
            out[:, h * HEAD_DIM : (h + 1) * HEAD_DIM] = (factor * (term[:, here] + more)).astype(BF16)


def finish(info, arrays, terms, pieces, outs, first, step, factor, behind):
    rows, width = arrays[0].shape
    heads = pieces[0].shape[1]
    columns = pl.BlockSpec((rows, step * HEAD_DIM), lambda i: (0, first // step + i))
    fixed = 1 + 4 + 4 + PARTS
    return pl.pallas_call(
        functools.partial(finish_kernel, first, step, factor),
        out_shape=[jax.ShapeDtypeStruct((rows, width), BF16)] * 4,
        grid=(heads // step,),
        in_specs=[SCALARS] + [WHOLE] * (8 + PARTS) + [LEFT] * (len(outs) + len(behind)),
        out_specs=[columns] * 4,
        scratch_shapes=[pltpu.VMEM((step, 2, HEAD_DIM, HEAD_DIM), BF16)],
        input_output_aliases={fixed + i: i for i in range(len(outs))},
        compiler_params=pltpu.CompilerParams(vmem_limit_bytes=SMALL_LIMIT),
    )(info, *arrays, *terms, *pieces, *outs, *behind)


def swap(array, size, mask):
    return lax.ppermute(array, "local", [(i, i ^ mask) for i in range(size)])


def local(query_rows, key_rows, value_rows, out_grad):
    arrays = (query_rows, key_rows, value_rows, out_grad)
    rows, width = query_rows.shape
    heads = width // HEAD_DIM
    size, nodes = lax.axis_size("local"), lax.axis_size("node")
    blocks = size // PARTS
    assert nodes == 2 and size % PARTS == 0 and sum(CHUNKS) == heads
    factor = 1.0 / math.sqrt(HEAD_DIM * rows * nodes * size)
    node, place_in = lax.axis_index("node"), lax.axis_index("local")
    info = (place_in * 2 + node).astype(jnp.int32).reshape(1)

    firsts = [sum(CHUNKS[:i]) for i in range(len(CHUNKS))]
    pieces, given, ready, state, terms = {}, {}, {}, {}, {}
    outs = ()
    last = None
    for stage, i in ORDER:
        first, count = firsts[i], CHUNKS[i]
        behind = [] if last is None else [last]
        if stage == "state":
            own = states(info, arrays, first, count, behind)
            last = own[0]
            got = {r: swap(own[r], size, r) for r in TURN[1:]}
            pieces[i] = [own[0], got[1], got[2], got[3]]
        elif stage == "sum":
            last, halves = block_sum(info, [pieces[i][r] for r in TURN], behind)
            across = lax.ppermute(halves, "node", [(0, 1), (1, 0)])
            state[i] = last, across
        elif stage == "offer":
            total, across = state[i]
            if blocks == 2:
                last = offer(info, total, across, behind)
                other = swap(last, size, PARTS)
                given[i] = [across, other, lax.ppermute(other, "node", [(0, 1), (1, 0)])]
            else:
                given[i] = [sums_outside(total, node, place_in // PARTS, blocks)]
        elif stage == "spread":
            own = spread(info, pieces[i], given[i], behind)
            last = own[0]
            got = {r: swap(own[r], size, r) for r in TURN_BACK[1:]}
            ready[i] = [own[0], got[1], got[2], got[3]]
        elif stage == "inner":
            terms[i] = inner(arrays, first, count, FINISH_STEP[i], behind)
            last = terms[i][0]
        else:
            outs = finish(
                info, arrays, terms[i], [ready[i][r] for r in TURN_BACK], outs, first, FINISH_STEP[i], factor, behind
            )
    return tuple(outs)


def solution(mesh):
    rows = P(("group", "node", "local"), None)
    return jax.shard_map(
        local, mesh=mesh, in_specs=(rows,) * 4, out_specs=(rows,) * 4, check_vma=False
    )
```

```python
import functools
import math

import jax
import jax.numpy as jnp
from jax import lax
from jax.experimental import pallas as pl
from jax.experimental.pallas import tpu as pltpu
from jax.sharding import PartitionSpec as P

HEAD_DIM = 128
PARTS = 4
QUARTER = HEAD_DIM // PARTS
CHUNKS = (8, 8)
STEP = 8
TURN = (0, 3, 2, 1)
TURN_BACK = (0, 3, 2, 1)
FINISH_STEP = (8, 8)
ORDER = (
    ("state", 0),
    ("state", 1),
    ("inner", 0),
    ("sum", 0),
    ("offer", 0),
    ("inner", 1),
    ("sum", 1),
    ("offer", 1),
    ("spread", 0),
    ("spread", 1),
    ("finish", 0),
    ("finish", 1),
)

F32 = jnp.float32
BF16 = jnp.bfloat16
VMEM_LIMIT = 16 * 1024 * 1024
SMALL_LIMIT = 16 * 1024 * 1024
STATE_LIMIT = 60 * 1024 * 1024

SCALARS = pl.BlockSpec(memory_space=pltpu.SMEM)
WHOLE = pl.BlockSpec(memory_space=pltpu.VMEM)
FAR = pl.BlockSpec(memory_space=pltpu.HBM)
LEFT = pl.BlockSpec(memory_space=pl.ANY)


def dot(a, b, ca, cb):
    return lax.dot_general(a, b, (((ca,), (cb,)), ((), ())), preferred_element_type=F32)


def unpack(info):
    return (info[0] >> 1) % PARTS, info[0] & 1, (info[0] >> 1) // PARTS


def place(info, r):
    return pl.multiple_of((info[0] ^ r) * QUARTER, QUARTER)


def state_kernel(first, heads, info, q, k, v, g, *refs):
    info = unpack(info)
    outs, (held, hold, sems) = refs[-PARTS - 3 : -3], refs[-3:]
    groups = [(at, min(STEP, heads - at)) for at in range(0, heads, STEP)]
    copies = []
    for n, (at, wide) in enumerate(groups):
        there = pl.ds((first + at) * HEAD_DIM, wide * HEAD_DIM)
        here = pl.ds(at * HEAD_DIM, wide * HEAD_DIM)
        copies.append(
            [
                pltpu.make_async_copy(ref.at[:, there], held.at[i, :, here], sems.at[n, i])
                for i, ref in enumerate((k, v, q, g))
            ]
        )
        for copy in copies[-1]:
            copy.start()
    for n, (at, wide) in enumerate(groups):
        for half in range(2):
            copies[n][2 * half].wait()
            copies[n][2 * half + 1].wait()
            for h in range(at, at + wide):
                cols = slice(h * HEAD_DIM, (h + 1) * HEAD_DIM)
                hold[half] = dot(held[2 * half, :, cols], held[2 * half + 1, :, cols], 0, 0)
                for r in range(PARTS):
                    outs[r][half, h] = hold[half, pl.ds(place(info, r), QUARTER), :]


def states(info, arrays, first, heads, behind):
    rows = arrays[0].shape[0]
    piece = jax.ShapeDtypeStruct((2, heads, QUARTER, HEAD_DIM), F32)
    return pl.pallas_call(
        functools.partial(state_kernel, first, heads),
        out_shape=[piece] * PARTS,
        in_specs=[SCALARS] + [FAR] * 4 + [LEFT] * len(behind),
        out_specs=[WHOLE] * PARTS,
        scratch_shapes=[
            pltpu.VMEM((4, rows, heads * HEAD_DIM), BF16),
            pltpu.VMEM((2, HEAD_DIM, HEAD_DIM), F32),
            pltpu.SemaphoreType.DMA((-(-heads // STEP), 4)),
        ],
        compiler_params=pltpu.CompilerParams(vmem_limit_bytes=STATE_LIMIT),
    )(info, *arrays, *behind)


def add_kernel(info, a, b, c, d, *refs):
    info = unpack(info)
    total, halves = refs[-2:]
    total[...] = (a[...] + b[...]) + (c[...] + d[...])
    halves[...] = total[info[1]]


def block_sum(info, pieces, behind):
    shape = pieces[0].shape
    return pl.pallas_call(
        add_kernel,
        out_shape=[jax.ShapeDtypeStruct(shape, F32), jax.ShapeDtypeStruct(shape[1:], F32)],
        in_specs=[SCALARS] + [WHOLE] * PARTS + [LEFT] * len(behind),
        out_specs=[WHOLE] * 2,
        compiler_params=pltpu.CompilerParams(vmem_limit_bytes=VMEM_LIMIT),
    )(info, *pieces, *behind)


def offer_kernel(info, total, across, *refs):
    info = unpack(info)
    out = refs[-1]
    node, upper = info[1], jnp.where(info[2] > 0, 1, 0)
    half = out.shape[1]
    for j in range(2):
        heads = slice(j * half, (j + 1) * half)
        out[j] = total[upper, heads] + jnp.where(node != upper, across[heads], 0.0)
    heads = pl.ds(node * half, half)
    out[2] = jnp.where(node == upper, across[heads], total[1 - upper, heads])


def offer(info, total, across, behind):
    heads = total.shape[1]
    return pl.pallas_call(
        offer_kernel,
        out_shape=jax.ShapeDtypeStruct((3, heads // 2, *total.shape[2:]), F32),
        in_specs=[SCALARS, WHOLE, WHOLE] + [LEFT] * len(behind),
        out_specs=WHOLE,
        compiler_params=pltpu.CompilerParams(vmem_limit_bytes=VMEM_LIMIT),
    )(info, total, across, *behind)


def spread_kernel(pair, info, *refs):
    info = unpack(info)
    count = 3 if pair else 1
    pieces, given, outs = refs[:PARTS], refs[PARTS : PARTS + count], refs[-PARTS:]
    mine, node, upper = info[0], info[1], jnp.where(info[2] > 0, 1, 0)
    half = pieces[0].shape[1] // 2
    for j in range(2):
        heads = slice(j * half, (j + 1) * half)
        if pair:
            across, here, there = given
            alone = node != upper
            main = here[j]
            extra = jnp.where(node == j, here[2], there[2])
            whole = across[heads] + jnp.where(alone, extra, main)
            part = jnp.where(alone, main, 0.0)
            prefix = jnp.where(node > 0, whole, part)
            suffix = jnp.where(node > 0, part, whole)
        else:
            prefix, suffix = given[0][0, heads], given[0][1, heads]
        for r in range(PARTS):
            before, after = prefix, suffix
            for other in range(PARTS):
                if other != r:
                    earlier = (mine ^ other) < (mine ^ r)
                    before = before + jnp.where(earlier, pieces[other][0, heads], 0.0)
                    after = after + jnp.where(earlier, 0.0, pieces[other][1, heads])
            outs[r][0, heads] = before
            outs[r][1, heads] = after


def spread(info, pieces, given, behind):
    return pl.pallas_call(
        functools.partial(spread_kernel, len(given) > 1),
        out_shape=[jax.ShapeDtypeStruct(pieces[0].shape, F32)] * PARTS,
        in_specs=[SCALARS] + [WHOLE] * (PARTS + len(given)) + [LEFT] * len(behind),
        out_specs=[WHOLE] * PARTS,
        compiler_params=pltpu.CompilerParams(vmem_limit_bytes=VMEM_LIMIT),
    )(info, *pieces, *given, *behind)


def sums_outside(total, node, block, blocks):
    everything = lax.all_gather(total, ("node", "local"))
    everything = everything.reshape(-1, blocks, PARTS, *total.shape)
    everything = lax.dynamic_index_in_dim(everything, lax.axis_index("local") % PARTS, 2, False)
    everything = everything.reshape(-1, *total.shape)
    at = node * blocks + block
    earlier = (jnp.arange(everything.shape[0]) < at)[:, None, None, None]
    later = (jnp.arange(everything.shape[0]) > at)[:, None, None, None]
    prefix = jnp.sum(jnp.where(earlier, everything[:, 0], 0.0), axis=0)
    suffix = jnp.sum(jnp.where(later, everything[:, 1], 0.0), axis=0)
    return jnp.stack([prefix, suffix])


def inner_kernel(first, step, q, k, v, g, *refs):
    att, qg, kg, vg = refs[-4:]
    rows = q.shape[0]
    after = lax.broadcasted_iota(jnp.int32, (rows, rows), 0)
    before = lax.broadcasted_iota(jnp.int32, (rows, rows), 1)
    start = pl.program_id(0) * step
    for h in range(step):
        cols = pl.ds(pl.multiple_of((first + start + h) * HEAD_DIM, HEAD_DIM), HEAD_DIM)
        here = pl.ds(pl.multiple_of((start + h) * HEAD_DIM, HEAD_DIM), HEAD_DIM)
        qh, kh, vh, gh = q[:, cols], k[:, cols], v[:, cols], g[:, cols]
        weights = jnp.where(after >= before, dot(qh, kh, 1, 1), 0.0).astype(BF16)
        grad_weights = jnp.where(after >= before, dot(gh, vh, 1, 1), 0.0).astype(BF16)
        att[:, here] = dot(weights, vh, 1, 0)
        qg[:, here] = dot(grad_weights, kh, 1, 0)
        kg[:, here] = dot(grad_weights, qh, 0, 0)
        vg[:, here] = dot(weights, gh, 0, 0)


def inner(arrays, first, heads, step, behind):
    rows = arrays[0].shape[0]
    return pl.pallas_call(
        functools.partial(inner_kernel, first, step),
        out_shape=[jax.ShapeDtypeStruct((rows, heads * HEAD_DIM), F32)] * 4,
        grid=(heads // step,),
        in_specs=[WHOLE] * 4 + [LEFT] * len(behind),
        out_specs=[WHOLE] * 4,
        compiler_params=pltpu.CompilerParams(vmem_limit_bytes=SMALL_LIMIT),
    )(*arrays, *behind)


def finish_kernel(first, step, factor, info, q, k, v, g, *refs):
    info = unpack(info)
    terms, pieces = refs[:4], refs[4 : 4 + PARTS]
    outs, hold = refs[-5:-1], refs[-1]
    start = pl.program_id(0) * step
    for h in range(step):
        cols = pl.ds(pl.multiple_of((first + start + h) * HEAD_DIM, HEAD_DIM), HEAD_DIM)
        here = pl.ds(pl.multiple_of((start + h) * HEAD_DIM, HEAD_DIM), HEAD_DIM)
        for r, piece in zip(TURN_BACK, pieces):
            at = pl.ds(place(info, r), QUARTER)
            hold[h, 0, at, :] = piece[0, start + h].astype(BF16)
            hold[h, 1, at, :] = piece[1, start + h].astype(BF16)
        prefix, suffix = hold[h, 0], hold[h, 1]
        outer = (
            dot(q[:, cols], prefix, 1, 0),
            dot(g[:, cols], prefix, 1, 1),
            dot(v[:, cols], suffix, 1, 1),
            dot(k[:, cols], suffix, 1, 0),
        )
        for out, term, more in zip(outs, terms, outer):
            out[:, h * HEAD_DIM : (h + 1) * HEAD_DIM] = (factor * (term[:, here] + more)).astype(BF16)


def finish(info, arrays, terms, pieces, outs, first, step, factor, behind):
    rows, width = arrays[0].shape
    heads = pieces[0].shape[1]
    columns = pl.BlockSpec((rows, step * HEAD_DIM), lambda i: (0, first // step + i))
    fixed = 1 + 4 + 4 + PARTS
    return pl.pallas_call(
        functools.partial(finish_kernel, first, step, factor),
        out_shape=[jax.ShapeDtypeStruct((rows, width), BF16)] * 4,
        grid=(heads // step,),
        in_specs=[SCALARS] + [WHOLE] * (8 + PARTS) + [LEFT] * (len(outs) + len(behind)),
        out_specs=[columns] * 4,
        scratch_shapes=[pltpu.VMEM((step, 2, HEAD_DIM, HEAD_DIM), BF16)],
        input_output_aliases={fixed + i: i for i in range(len(outs))},
        compiler_params=pltpu.CompilerParams(vmem_limit_bytes=SMALL_LIMIT),
    )(info, *arrays, *terms, *pieces, *outs, *behind)


def swap(array, size, mask):
    return lax.ppermute(array, "local", [(i, i ^ mask) for i in range(size)])


def local(query_rows, key_rows, value_rows, out_grad):
    arrays = (query_rows, key_rows, value_rows, out_grad)
    rows, width = query_rows.shape
    heads = width // HEAD_DIM
    size, nodes = lax.axis_size("local"), lax.axis_size("node")
    blocks = size // PARTS
    assert nodes == 2 and size % PARTS == 0 and sum(CHUNKS) == heads
    factor = 1.0 / math.sqrt(HEAD_DIM * rows * nodes * size)
    node, place_in = lax.axis_index("node"), lax.axis_index("local")
    info = (place_in * 2 + node).astype(jnp.int32).reshape(1)

    firsts = [sum(CHUNKS[:i]) for i in range(len(CHUNKS))]
    pieces, given, ready, state, terms = {}, {}, {}, {}, {}
    outs = ()
    last = None
    for stage, i in ORDER:
        first, count = firsts[i], CHUNKS[i]
        behind = [] if last is None else [last]
        if stage == "state":
            own = states(info, arrays, first, count, behind)
            last = own[0]
            got = {r: swap(own[r], size, r) for r in TURN[1:]}
            pieces[i] = [own[0], got[1], got[2], got[3]]
        elif stage == "sum":
            last, halves = block_sum(info, [pieces[i][r] for r in TURN], behind)
            across = lax.ppermute(halves, "node", [(0, 1), (1, 0)])
            state[i] = last, across
        elif stage == "offer":
            total, across = state[i]
            if blocks == 2:
                last = offer(info, total, across, behind)
                other = swap(last, size, PARTS)
                given[i] = [across, other, lax.ppermute(other, "node", [(0, 1), (1, 0)])]
            else:
                given[i] = [sums_outside(total, node, place_in // PARTS, blocks)]
        elif stage == "spread":
            own = spread(info, pieces[i], given[i], [])
            last = own[0]
            got = {r: swap(own[r], size, r) for r in TURN_BACK[1:]}
            ready[i] = [own[0], got[1], got[2], got[3]]
        elif stage == "inner":
            terms[i] = inner(arrays, first, count, FINISH_STEP[i], behind)
            last = terms[i][0]
        else:
            outs = finish(
                info, arrays, terms[i], [ready[i][r] for r in TURN_BACK], outs, first, FINISH_STEP[i], factor, []
            )
    return tuple(outs)


def solution(mesh):
    rows = P(("group", "node", "local"), None)
    return jax.shard_map(
        local, mesh=mesh, in_specs=(rows,) * 4, out_specs=(rows,) * 4, check_vma=False
    )
```
